256 devices in a mesh: rep: 16 (over y, z_lo), row: 16 (over x, z_hi, core).
Axes of the slice: x: 4, y: 4, z: 8 (z_hi: 2, z_lo: 4; z = z_hi * 4 + z_lo), core: 2. Of those that a mesh axis runs over, the one named last changes fastest.
Arguments:
- features: bfloat16 [16, 6144, 256], P('rep', 'row'), may hold values from -6 to 6
- weight: bfloat16 [256, 256], replicated, may hold values from -0.375 to 0.375
- block_cols: int32 [16, 768, 3], P('rep', 'row'), may hold values from 0 to 47
- edge_counts: int32 [16, 768, 3, 128, 128], P('rep', 'row'), may hold values from 0 to 5
- cotangent: bfloat16 [16, 6144, 256], P('row', 'rep'), may hold values from -6 to 6
Outputs:
- activated: bfloat16 [16, 6144, 256], P('row', 'rep')
- grad_features: bfloat16 [16, 6144, 256], P('rep', 'row')
- grad_weight: float32 [256, 256], replicated
The draws below stay inside these ranges and needn't reach their ends.
Inputs may be any that keep to these rules, and one draw needn't show every extreme that they name: `block_cols`: a block row may name the same column tile more than once.
All inputs are finite; a program needn't handle non-finite values.
Results may differ from the reference program's by a relative error of at most 0.0063.
Values may be sent and summed in bfloat16 or wider, within the bound.
A program may use at most 128 MiB of HBM per device.

```python
import math
import jax
import jax.numpy as jnp
import numpy as np
from jax import lax

FEATURES = 256
TILE_SIZE = 128
ROW_BLOCKS = 3
ROW_SLABS = 16
COLUMN_SLABS = 16
SLAB_TILES = 48
SLAB_ROWS = 6144
COL_TILES = 48
COL_NODES = 6144


def draw_edge_counts(key, part):
    key = jax.random.fold_in(key, 11)
    first, second, third = jax.random.split(key, 3)
    shape = (COLUMN_SLABS, ROW_SLABS * SLAB_TILES, ROW_BLOCKS, TILE_SIZE, TILE_SIZE)
    slab_index = lax.broadcasted_iota(jnp.int32, shape, 0)
    level = 1 + 4 * slab_index // (COLUMN_SLABS - 1)
    row_level = jax.random.randint(first, shape[:4] + (1,), 1, 4)
    keep = (jax.random.randint(second, shape, 0, 4) < row_level).astype(jnp.int32)
    amount = jax.random.randint(third, shape, 1, level + 1)
    return keep * amount


def plant(drawn, own_key, smallest, top_value):
    place = [jax.random.randint(jax.random.fold_in(own_key, axis), (), 0, length) for axis, length in enumerate(drawn.shape)]
    main_axis = drawn.shape.index(max(drawn.shape))
    beside = place[:main_axis] + [(place[main_axis] + 1) % drawn.shape[main_axis]] + place[main_axis + 1:]
    return drawn.at[tuple(place)].set(smallest).at[tuple(beside)].set(top_value)


def block_levels(rng, dims, pieces, smallest, largest):
    gain = 1.0
    for dim, blocks in pieces:
        steps = jax.random.uniform(jax.random.fold_in(jax.random.fold_in(rng, 6), dim), (blocks,), jnp.float32, smallest / len(pieces), largest / len(pieces))
        gain = gain * jnp.repeat(jnp.exp(steps), dims[dim] // blocks).reshape((-1,) + (1,) * (len(dims) - 1 - dim))
    return gain


def rank_table(count, slope):
    portions = [(1 << 20) // math.isqrt(standing ** slope) + 1 for standing in range(1, count + 1)]
    deviation = 1 + sum(portions) // (1 << 30)
    return np.cumsum(np.array([max(1, weight // deviation) for weight in portions]))


def skewed_ids(stream_key, extent, number_of, slope):
    table = rank_table(number_of, slope)
    ticket = jax.random.randint(jax.random.fold_in(stream_key, 1), extent, 0, int(table[number_of - 1]))
    rank = jnp.searchsorted(jnp.asarray(table, jnp.int32), ticket, side="right")
    return jax.random.permutation(jax.random.fold_in(stream_key, 2), number_of)[rank].astype(jnp.int32)


def centred(key, extent, width, most, cuts=(), dtype=jnp.bfloat16):
    gain = block_levels(key, extent, cuts, -0.22, 0.18) if cuts else 1.0
    drawn = jax.random.normal(key, extent, jnp.float32) * width * gain
    return jnp.minimum(jnp.maximum(drawn, -most), most).astype(dtype)


def setup_inputs(seed: int = 0) -> dict:
    key_list = jax.random.split(jax.random.key(seed), 6)
    return {
        "features": centred(key_list[0], (COLUMN_SLABS, COL_NODES, FEATURES), 1.0, 6.0, ((0, 16), (1, 16))),
        "weight": centred(key_list[1], (FEATURES, FEATURES), FEATURES ** -0.5, 0.375),
        "block_cols": plant(skewed_ids(key_list[2], (COLUMN_SLABS, ROW_SLABS * SLAB_TILES, ROW_BLOCKS), COL_TILES, 2), jax.random.fold_in(key_list[2], 3), 0, COL_TILES - 1).astype(jnp.int32),
        "edge_counts": draw_edge_counts(jax.random.fold_in(key_list[5], 71), 0),
        "cotangent": centred(key_list[4], (ROW_SLABS, SLAB_ROWS, FEATURES), 1.0, 6.0, ((0, 16), (1, 16))),
    }


def reference(features, weight, block_cols, edge_counts, cotangent):
    tile_size = edge_counts.shape[-1]
    feat_width = features.shape[-1]
    block_rows = block_cols.shape[1]
    col_tiles = features.shape[1] // tile_size

    def forward_step(carry, slab):
        feats, columns, counts = slab
        feat_tiles = feats.reshape(col_tiles, tile_size, feat_width).astype(jnp.float32)
        picked = feat_tiles[columns]
        term = jnp.einsum('rkij,rkjf->rif', counts.astype(jnp.float32), picked)
        row_terms = lax.optimization_barrier(jnp.sum(counts, axis=(1, 3))).astype(jnp.float32)
        return ((carry[0] + term, carry[1] + row_terms), None)
    init = (jnp.zeros((block_rows, tile_size, feat_width), jnp.float32), jnp.zeros((block_rows, tile_size), jnp.float32))
    (summed, rowsum), _ = lax.scan(forward_step, init, (features, block_cols, edge_counts))
    row_scale = lax.rsqrt(1.0 + rowsum.reshape(-1))
    aggregated = (summed.reshape(-1, feat_width) * row_scale[:, None]).astype(jnp.bfloat16)
    preact = jnp.dot(aggregated, weight, preferred_element_type=jnp.float32)
    gate_value = jax.nn.sigmoid(preact)
    activated = (preact * gate_value).astype(jnp.bfloat16)
    grad_rows = cotangent.reshape(-1, feat_width).astype(jnp.float32)
    grad_pre = (grad_rows * gate_value * (1.0 + preact * (1.0 - gate_value))).astype(jnp.bfloat16)
    grad_weight = jnp.dot(aggregated.T, grad_pre, preferred_element_type=jnp.float32)
    scaled_grad = (jnp.dot(grad_pre, weight.T, preferred_element_type=jnp.float32) * row_scale[:, None]).astype(jnp.bfloat16)
    grad_tiles = scaled_grad.reshape(block_rows, tile_size, feat_width).astype(jnp.float32)

    def backward_step(slab):
        columns, counts = slab
        contrib = jnp.einsum('rkij,rif->rkjf', counts.astype(jnp.float32), grad_tiles)
        col_sum = jax.ops.segment_sum(contrib.reshape(-1, tile_size, feat_width), columns.reshape(-1).astype(jnp.int32), num_segments=col_tiles)
        return col_sum.reshape(-1, feat_width).astype(jnp.bfloat16)
    grad_features = lax.map(backward_step, (block_cols, edge_counts))
    return (activated.reshape(cotangent.shape), grad_features, grad_weight)
```

```python
import jax
import jax.numpy as jnp
from jax import lax
from jax.experimental import pallas as pl
from jax.experimental.pallas import tpu as pltpu
from jax.sharding import PartitionSpec as P

BF16 = jnp.bfloat16
F32 = jnp.float32
MESH = pl.DeviceIdType.MESH
TILE = 128
HALVES = 2
MESSAGES = 160


def order_by_column(columns):
    flat = columns.reshape(-1)
    entry = jnp.arange(flat.shape[0])
    tile = jnp.arange(48)
    before = (flat[None, :] < flat[:, None]) | (
        (flat[None, :] == flat[:, None]) & (entry[None, :] < entry[:, None])
    )
    rank = jnp.sum(before, axis=1)
    onehot = rank[:, None] == entry[None, :]
    perm = jnp.sum(jnp.where(onehot, entry[:, None], 0), axis=0).astype(jnp.int32)
    smaller = jnp.sum(flat[None, :] < flat[:, None], axis=1)
    first = jnp.sum(jnp.where(onehot, (smaller == rank)[:, None], False), axis=0)
    same = 1.0 - first.astype(F32)
    upto = jnp.sum(flat[:, None] <= tile[None, :], axis=0)
    last = jnp.maximum(upto - 1, 0).astype(jnp.int32)
    used = jnp.any(flat[:, None] == tile[None, :], axis=0).astype(F32)
    return flat, perm, same, last, used


def kernel(
    cols, perm, same, last, used, feat_in, weight, cot, counts_hbm,
    act_out, gf_out, gw_out,
    raw, cnt, cnt_t, feats0, feats1, psend0, psend1, yrel, yfin, zsend, zrecv,
    slab0, slab1, prefix, acc, cout0, cout1, corer, xs, xrel, xfin, keep, zfs, zfr,
    deg_send, deg_y, deg_zs, deg_z, agg, gpre,
    wp, g_core, g1, g_x, g2, g_zh, g3, g_y, g4, g_zl, gw_full,
    load_sem, send_sem, recv_sem,
):
    rep = lax.axis_index("rep")
    row = lax.axis_index("row")
    y, zl = rep // 4, rep % 4
    x, zh, c = row // 4, (row // 2) % 2, row % 2
    feats, psend, slab, cout = (
        (feats0, feats1), (psend0, psend1), (slab0, slab1), (cout0, cout1)
    )

    def device(x_=x, y_=y, zl_=zl, zh_=zh, c_=c):
        return (y_ * 4 + zl_, x_ * 4 + zh_ * 2 + c_)

    xp, xm, xo = (x + 1) % 4, (x + 3) % 4, (x + 2) % 4
    yp, ym, yo = (y + 1) % 4, (y + 3) % 4, (y + 2) % 4
    zn = [(zl + d) % 4 for d in range(4)]
    to_xp, to_xm, to_xo = device(x_=xp), device(x_=xm), device(x_=xo)
    to_yp, to_ym, to_yo = device(y_=yp), device(y_=ym), device(y_=yo)
    to_z = [None] + [device(zl_=zn[d]) for d in (1, 2, 3)]
    to_zh = device(zh_=1 - zh)
    to_core = device(c_=1 - c)
    partners = [to_xp, to_xm, to_xo, to_yp, to_ym, to_yo, *to_z[1:], to_zh, to_core]

    sent = {}

    def send(name, src, dst, target):
        slot = len(sent)
        copy = pltpu.make_async_remote_copy(
            src_ref=src, dst_ref=dst, send_sem=send_sem.at[slot], recv_sem=recv_sem.at[slot],
            device_id=target, device_id_type=MESH,
        )
        copy.start()
        sent[name] = copy

    def arrived(name):
        sent[name].wait_recv()

    loads = []
    for i in range(16):
        piece = pl.ds(3 * i, 3)
        load = pltpu.make_async_copy(counts_hbm.at[piece], raw.at[piece], load_sem.at[i])
        load.start()
        loads.append(load)

    barrier = pltpu.get_barrier_semaphore()
    for partner in partners:
        pl.semaphore_signal(barrier, inc=1, device_id=partner, device_id_type=MESH)

    def block(ref, index):
        return ref.at[pl.ds(3 * index, 3)]

    own_row = x * 4 + zh * 2 + c
    for h in range(HALVES):
        feats[h][pl.ds(3 * own_row, 3)] = feat_in[:, :, h * TILE : (h + 1) * TILE]
    pl.semaphore_wait(barrier, len(partners))

    def gather_start(h):
        mine = block(feats[h], own_row)
        send(("xp", h), mine, mine, to_xp)
        send(("xm", h), mine, mine, to_xm)
        send(("zh", h), mine, mine, to_zh)
        send(("c0", h), mine, mine, to_core)

    def row_index(x_, zh_):
        return x_ * 4 + zh_ * 2 + c

    def gather_near(h):
        arrived(("xp", h))
        left = block(feats[h], row_index(xm, zh))
        send(("xp2", h), left, left, to_xp)
        send(("c1", h), left, left, to_core)
        arrived(("xm", h))
        right = block(feats[h], row_index(xp, zh))
        send(("c2", h), right, right, to_core)

    def gather_far(h):
        arrived(("zh", h))
        other = block(feats[h], row_index(x, 1 - zh))
        send(("zxp", h), other, other, to_xp)
        send(("zxm", h), other, other, to_xm)
        send(("c3", h), other, other, to_core)

    def gather_near2(h):
        arrived(("xp2", h))
        oppo = block(feats[h], row_index(xo, zh))
        send(("c4", h), oppo, oppo, to_core)

    def gather_far2(h):
        arrived(("zxm", h))
        right = block(feats[h], row_index(xp, 1 - zh))
        send(("zxm2", h), right, right, to_xm)
        send(("c5", h), right, right, to_core)
        arrived(("zxp", h))
        left = block(feats[h], row_index(xm, 1 - zh))
        send(("c6", h), left, left, to_core)

    def gather_end(h):
        arrived(("zxm2", h))
        oppo = block(feats[h], row_index(xo, 1 - zh))
        send(("c7", h), oppo, oppo, to_core)
        for i in range(8):
            arrived(("c%d" % i, h))

    def convert(first, end):
        for i in range(first, end):
            loads[i].wait()
            for t in range(3):
                total = None
                for k in range(3):
                    tile = raw[3 * i + t, k].astype(F32)
                    cnt[3 * i + t, :, k * TILE : (k + 1) * TILE] = tile.astype(BF16)
                    turned = tile.T
                    cnt_t[9 * i + 3 * t + k] = turned.astype(BF16)
                    part = jnp.sum(turned, axis=0, keepdims=True)
                    total = part if total is None else total + part
                deg_send[i // 4, i % 4, t : t + 1] = total

    def forward(h, target):
        def step(i, carry):
            r = target * 12 + i
            picked = jnp.concatenate([feats[h][cols[3 * r + k]] for k in range(3)], axis=0)
            psend[h][r] = jnp.dot(cnt[r], picked, preferred_element_type=F32).astype(BF16)
            return carry

        lax.fori_loop(0, 12, step, 0, unroll=12)

    def pair(h, target, which):
        return psend[h].at[pl.ds(target * 12 + 6 * which, 6)]

    def add_into(ref, where, other):
        ref[where] = (ref[where].astype(F32) + other.astype(F32)).astype(BF16)

    def reduce_start(h):
        forward(h, yo)
        send(("yr0", h), pair(h, yo, 0), yrel.at[h, 0], to_yp)
        send(("yr1", h), pair(h, yo, 1), yrel.at[h, 1], to_ym)

    def reduce_near(h):
        forward(h, yp)
        send(("yu0", h), pair(h, yp, 1), yfin.at[h, 0, 1], to_yp)
        forward(h, ym)
        send(("yu1", h), pair(h, ym, 0), yfin.at[h, 1, 0], to_ym)

    def reduce_relay(h):
        arrived(("yr0", h))
        add_into(psend[h], pl.ds(yp * 12, 6), yrel[h, 0])
        send(("yc0", h), pair(h, yp, 0), yfin.at[h, 0, 0], to_yp)
        arrived(("yr1", h))
        add_into(psend[h], pl.ds(ym * 12 + 6, 6), yrel[h, 1])
        send(("yc1", h), pair(h, ym, 1), yfin.at[h, 1, 1], to_ym)

    def reduce_z(h):
        for name in ("yu0", "yu1", "yc0", "yc1"):
            arrived((name, h))
        for which in range(2):
            mine = psend[h][pl.ds(y * 12 + 6 * which, 6)].astype(F32)
            total = mine + yfin[h, 0, which].astype(F32) + yfin[h, 1, which].astype(F32)
            zsend[h, pl.ds(2 * which, 2)] = total.astype(BF16).reshape(2, 3, TILE, TILE)
        for d in (1, 2, 3):
            send(("rz%d" % d, h), zsend.at[h, zn[d]], zrecv.at[h, zl], to_z[d])

    def degree_start():
        deg_y[y] = deg_send[y]
        for name, target, index in (("dp", to_yp, yp), ("dm", to_ym, ym), ("do", to_yo, yo)):
            send(name, deg_send.at[index], deg_y.at[y], target)

    def degree_z():
        for name in ("dp", "dm", "do"):
            arrived(name)
        deg_zs[...] = deg_y[0] + deg_y[1] + deg_y[2] + deg_y[3]
        deg_z[zl] = deg_zs[zl]
        for d in (1, 2, 3):
            send("dz%d" % d, deg_zs.at[zn[d]], deg_z.at[zl], to_z[d])

    def degree_end():
        for d in (1, 2, 3):
            arrived("dz%d" % d)
        total = deg_z[0] + deg_z[1] + deg_z[2] + deg_z[3]
        return lax.rsqrt(1.0 + total)

    own_rep = y * 4 + zl

    def dense(scale):
        for h in range(HALVES):
            for d in (1, 2, 3):
                arrived(("rz%d" % d, h))
        for t in range(3):
            column = jnp.broadcast_to(scale[t : t + 1], (TILE, TILE)).T
            halves = []
            for h in range(HALVES):
                total = zsend[h, zl, t].astype(F32)
                for d in (1, 2, 3):
                    total = total + zrecv[h, zn[d], t].astype(F32)
                halves.append((total * column).astype(BF16))
            aggregated = jnp.concatenate(halves, axis=1)
            rows = pl.ds(t * TILE, TILE)
            agg[rows] = aggregated
            preact = jnp.dot(aggregated, weight[...], preferred_element_type=F32)
            gate = jax.nn.sigmoid(preact)
            act_out[rows] = (preact * gate).astype(BF16)
            grad = (cot[rows].astype(F32) * gate * (1.0 + preact * (1.0 - gate))).astype(BF16)
            gpre[rows] = grad
            back = lax.dot_general(
                grad, weight[...], (((1,), (1,)), ((), ())), preferred_element_type=F32
            )
            for h in range(HALVES):
                part = back[:, h * TILE : (h + 1) * TILE] * column
                slab[h][3 * own_rep + t] = part.astype(BF16)

    def spread_start(h):
        mine = block(slab[h], own_rep)
        send(("sp0", h), mine, mine, to_yp)
        send(("sm0", h), mine, mine, to_ym)
        for d in (1, 2, 3):
            send(("sz%d" % d, h), mine, mine, to_z[d])

    def spread_z(h, d):
        arrived(("sz%d" % d, h))
        got = block(slab[h], y * 4 + zn[4 - d])
        send(("sp%d" % d, h), got, got, to_yp)
        send(("sm%d" % d, h), got, got, to_ym)

    def spread_y(h, d):
        source = zl if d == 0 else zn[4 - d]
        arrived(("sp%d" % d, h))
        if d % 2 == 0:
            got = block(slab[h], ym * 4 + source)
            send(("sf%d" % d, h), got, got, to_yp)
        arrived(("sm%d" % d, h))
        if d % 2 == 1:
            got = block(slab[h], yp * 4 + source)
            send(("sf%d" % d, h), got, got, to_ym)

    def spread_end(h):
        for d in range(4):
            arrived(("sf%d" % d, h))

    def backward(h, first, end):
        def step(i, carry):
            e = perm[i]
            part = jnp.dot(cnt_t[e], slab[h][e // 3], preferred_element_type=F32)
            total = acc[...] * same[i] + part
            acc[...] = total
            prefix[i] = total.astype(BF16)
            return carry

        lax.fori_loop(first, end, step, 0, unroll=12)

    def collect(h):
        def step(i, carry):
            for t in range(3):
                j = 3 * i + t
                tile = prefix[last[j]].astype(F32) * used[j]
                cout[h][i // 2, i % 2, t] = tile.astype(BF16)
            return carry

        lax.fori_loop(0, 16, step, 0, unroll=4)

    def core_start(h):
        for name, x_ in (("o", xo), ("p", xp), ("m", xm), ("s", x)):
            send(
                ("k" + name, h), cout[h].at[pl.ds(2 * x_, 2), 1 - c],
                corer.at[h, pl.ds(2 * x_, 2)], to_core,
            )

    def core_sum(h, name, x_):
        arrived(("k" + name, h))
        pieces = pl.ds(2 * x_, 2)
        total = cout[h][pieces, c].astype(F32) + corer[h, pieces].astype(F32)
        xs[h, pieces] = total.astype(BF16)

    def cross_start(h):
        core_sum(h, "o", xo)
        send(("xr0", h), xs.at[h, 2 * xo], xrel.at[h, 0], to_xp)
        send(("xr1", h), xs.at[h, 2 * xo + 1], xrel.at[h, 1], to_xm)
        core_sum(h, "p", xp)
        send(("xu0", h), xs.at[h, 2 * xp + 1], xfin.at[h, 0, 1], to_xp)
        core_sum(h, "m", xm)
        send(("xu1", h), xs.at[h, 2 * xm], xfin.at[h, 1, 0], to_xm)
        core_sum(h, "s", x)

    def cross_relay(h):
        arrived(("xr0", h))
        add_into(xs, (h, 2 * xp), xrel[h, 0])
        send(("xc0", h), xs.at[h, 2 * xp], xfin.at[h, 0, 0], to_xp)
        arrived(("xr1", h))
        add_into(xs, (h, 2 * xm + 1), xrel[h, 1])
        send(("xc1", h), xs.at[h, 2 * xm + 1], xfin.at[h, 1, 1], to_xm)

    def cross_sum(h, which):
        return (
            xs[h, 2 * x + which].astype(F32)
            + xfin[h, 0, which].astype(F32)
            + xfin[h, 1, which].astype(F32)
        )

    def cross_z(h):
        for name in ("xu0", "xu1", "xc0", "xc1"):
            arrived((name, h))
        zfs[h] = cross_sum(h, 1 - zh).astype(BF16)
        send(("fz", h), zfs.at[h], zfr.at[h], to_zh)
        keep[h] = cross_sum(h, zh)

    def cross_end(h):
        arrived(("fz", h))
        total = keep[h] + zfr[h].astype(F32)
        gf_out[:, :, h * TILE : (h + 1) * TILE] = total.astype(BF16)

    def gw_start():
        part = lax.dot_general(
            agg[...], gpre[...], (((0,), (0,)), ((), ())), preferred_element_type=F32
        )
        wp[...] = part.reshape(2, 4, 2, 16, 256)
        send("gc", wp.at[1 - c], g_core, to_core)

    def gw_x():
        arrived("gc")
        g1[...] = wp[c] + g_core[...]
        g_x[x] = g1[x]
        for name, target, x_ in (("gxp", to_xp, xp), ("gxm", to_xm, xm), ("gxo", to_xo, xo)):
            send(name, g1.at[x_], g_x.at[x], target)

    def gw_zh():
        for name in ("gxp", "gxm", "gxo"):
            arrived(name)
        g2[...] = g_x[0] + g_x[1] + g_x[2] + g_x[3]
        send("gzh", g2.at[1 - zh], g_zh, to_zh)

    def gw_y():
        arrived("gzh")
        g3[...] = g2[zh] + g_zh[...]
        g_y[y] = g3[...]
        for name, target in (("gyp", to_yp), ("gym", to_ym), ("gyo", to_yo)):
            send(name, g3, g_y.at[y], target)

    def gw_zl():
        for name in ("gyp", "gym", "gyo"):
            arrived(name)
        g4[...] = g_y[0] + g_y[1] + g_y[2] + g_y[3]
        g_zl[zl] = g4[...]
        for d in (1, 2, 3):
            send("gzl%d" % d, g4, g_zl.at[zl], to_z[d])

    def gw_back_zh():
        for d in (1, 2, 3):
            arrived("gzl%d" % d)
        gw_full[c, x, zh] = g_zl[0] + g_zl[1] + g_zl[2] + g_zl[3]
        mine = gw_full.at[c, x, zh]
        send("bzh", mine, mine, to_zh)

    def gw_back_x():
        arrived("bzh")
        mine = gw_full.at[c, x]
        for name, target in (("bxp", to_xp), ("bxm", to_xm), ("bxo", to_xo)):
            send(name, mine, mine, target)

    def gw_back_core():
        for name in ("bxp", "bxm", "bxo"):
            arrived(name)
        mine = gw_full.at[c]
        send("bc", mine, mine, to_core)

    def gw_end():
        arrived("bc")
        gw_out[...] = gw_full[...].reshape(256, 256)

    gather_start(0)
    gather_start(1)
    convert(0, 5)
    gather_near(0)
    convert(5, 10)
    gather_near2(0)
    gather_near(1)
    gather_far(0)
    convert(10, 16)
    degree_start()
    gather_near2(1)
    gather_far2(0)
    degree_z()
    gather_far(1)
    gather_end(0)

    reduce_start(0)
    gather_far2(1)
    reduce_near(0)
    forward(0, y)
    gather_end(1)
    reduce_start(1)
    reduce_relay(0)
    reduce_near(1)
    forward(1, y)
    scale = degree_end()
    reduce_z(0)
    reduce_relay(1)
    reduce_z(1)
    dense(scale)

    spread_start(0)
    spread_start(1)
    gw_start()
    acc[...] = jnp.zeros_like(acc)
    spread_y(0, 0)
    spread_z(0, 1)
    spread_y(1, 0)
    gw_x()
    spread_z(0, 2)
    spread_y(0, 1)
    spread_z(0, 3)
    spread_y(0, 2)
    gw_zh()
    spread_z(1, 1)
    spread_y(0, 3)
    spread_z(1, 2)
    spread_end(0)
    backward(0, 0, 72)
    spread_y(1, 1)
    spread_z(1, 3)
    backward(0, 72, 144)
    collect(0)
    core_start(0)
    spread_y(1, 2)
    cross_start(0)
    gw_y()
    spread_y(1, 3)
    cross_relay(0)
    spread_end(1)
    backward(1, 0, 72)
    gw_zl()
    backward(1, 72, 108)
    cross_z(0)
    backward(1, 108, 144)
    collect(1)
    core_start(1)
    gw_back_zh()
    cross_start(1)
    gw_back_x()
    cross_relay(1)
    gw_back_core()
    cross_end(0)
    cross_z(1)
    gw_end()
    cross_end(1)
    for copy in sent.values():
        copy.wait_send()


def shards(features, weight, block_cols, edge_counts, cotangent):
    cols, perm, same, last, used = order_by_column(block_cols[0])
    vmem = pl.BlockSpec(memory_space=pltpu.VMEM)
    smem = pl.BlockSpec(memory_space=pltpu.SMEM)
    slab = pltpu.VMEM((48, TILE, TILE), BF16)

    def tiles(*lead, dtype=BF16):
        return pltpu.VMEM((*lead, TILE, TILE), dtype)

    def floats(*shape):
        return pltpu.VMEM(shape, F32)

    activated, grad_features, grad_weight = pl.pallas_call(
        kernel,
        out_shape=(
            jax.ShapeDtypeStruct((384, 256), BF16),
            jax.ShapeDtypeStruct((3, TILE, 256), BF16),
            jax.ShapeDtypeStruct((256, 256), F32),
        ),
        in_specs=[smem] * 5 + [vmem] * 3 + [pl.BlockSpec(memory_space=pl.ANY)],
        out_specs=(vmem, vmem, vmem),
        scratch_shapes=[
            tiles(48, 3, dtype=jnp.int32),
            pltpu.VMEM((48, TILE, 3 * TILE), BF16),
            tiles(144),
            slab, slab, slab, slab,
            tiles(2, 2, 6),
            tiles(2, 2, 2, 6),
            tiles(2, 4, 3), tiles(2, 4, 3),
            slab, slab,
            tiles(144),
            floats(TILE, TILE),
            tiles(8, 2, 3), tiles(8, 2, 3),
            tiles(2, 8, 3), tiles(2, 8, 3),
            tiles(2, 2, 3), tiles(2, 2, 2, 3),
            tiles(2, 3, dtype=F32), tiles(2, 3), tiles(2, 3),
            floats(4, 4, 8, TILE), floats(4, 4, 8, TILE),
            floats(4, 8, TILE), floats(4, 8, TILE),
            pltpu.VMEM((384, 256), BF16), pltpu.VMEM((384, 256), BF16),
            floats(2, 4, 2, 16, 256),
            floats(4, 2, 16, 256), floats(4, 2, 16, 256),
            floats(4, 2, 16, 256), floats(2, 16, 256),
            floats(16, 256), floats(16, 256),
            floats(4, 16, 256), floats(16, 256),
            floats(4, 16, 256),
            floats(2, 4, 2, 16, 256),
            pltpu.SemaphoreType.DMA((16,)),
            pltpu.SemaphoreType.DMA((MESSAGES,)),
            pltpu.SemaphoreType.DMA((MESSAGES,)),
        ],
        compiler_params=pltpu.CompilerParams(
            collective_id=0, has_side_effects=True, vmem_limit_bytes=60 << 20
        ),
        name="graph_layer",
    )(
        cols, perm, same, last, used,
        features[0].reshape(3, TILE, 256), weight, cotangent[0], edge_counts[0],
    )
    return activated[None], grad_features.reshape(1, 384, 256), grad_weight


def solution(mesh):
    placed = (
        P("rep", "row", None),
        P(),
        P("rep", "row", None),
        P("rep", "row", None, None, None),
        P("row", "rep", None),
    )
    return jax.shard_map(
        shards,
        mesh=mesh,
        in_specs=placed,
        out_specs=(P("row", "rep", None), P("rep", "row", None), P()),
        check_vma=False,
    )
```

```python
import jax
import jax.numpy as jnp
from jax import lax
from jax.experimental import pallas as pl
from jax.experimental.pallas import tpu as pltpu
from jax.sharding import PartitionSpec as P

BF16 = jnp.bfloat16
F32 = jnp.float32
MESH = pl.DeviceIdType.MESH
TILE = 128
HALVES = 2
MESSAGES = 192
SUM_PARTS = ((0, 0, 3), (1, 0, 1), (1, 1, 2))
SPREAD_PARTS = ((0, 0, 1), (1, 0, 1), (0, 1, 2), (1, 1, 2))


def kernel(
    cols, cols_in, feat_hbm, weight_hbm, cot_hbm, counts_hbm,
    act_hbm, gf_hbm, gw_hbm,
    raw, cnt, cnt_t, feats0, feats1, psend0, psend1, pown, yrel, yfin, zsend, zown, zrecv,
    slab0, slab1, prefix, acc, cout0, cout1, corer, xs, xown, xfin, keep, zfs, zfr,
    deg_send, deg_y, deg_zs, deg_z, weight, cot, act, agg, gpre, gf,
    wp, g_core, g1, g_x, g2, g_zh, g3, g_y, g4, g_zl, gw_full,
    order_v, flag_v, order, flag,
    load_sem, late_sem, send_sem, recv_sem,
):
    rep = lax.axis_index("rep")
    row = lax.axis_index("row")
    y, zl = rep // 4, rep % 4
    x, zh, c = row // 4, (row // 2) % 2, row % 2
    feats, psend, slab, cout = (
        (feats0, feats1), (psend0, psend1), (slab0, slab1), (cout0, cout1)
    )

    def device(x_=x, y_=y, zl_=zl, zh_=zh, c_=c):
        return (y_ * 4 + zl_, x_ * 4 + zh_ * 2 + c_)

    xp, xm, xo = (x + 1) % 4, (x + 3) % 4, (x + 2) % 4
    yp, ym, yo = (y + 1) % 4, (y + 3) % 4, (y + 2) % 4
    zn = [(zl + d) % 4 for d in range(4)]
    to_xp, to_xm, to_xo = device(x_=xp), device(x_=xm), device(x_=xo)
    to_yp, to_ym, to_yo = device(y_=yp), device(y_=ym), device(y_=yo)
    to_z = [None] + [device(zl_=zn[d]) for d in (1, 2, 3)]
    to_zh = device(zh_=1 - zh)
    to_core = device(c_=1 - c)
    partners = [to_xp, to_xm, to_xo, to_yp, to_ym, to_yo, *to_z[1:], to_zh, to_core]

    sent = {}

    def send(name, src, dst, target):
        slot = len(sent)
        copy = pltpu.make_async_remote_copy(
            src_ref=src, dst_ref=dst, send_sem=send_sem.at[slot], recv_sem=recv_sem.at[slot],
            device_id=target, device_id_type=MESH,
        )
        copy.start()
        sent[name] = copy

    def arrived(name):
        sent[name].wait_recv()

    barrier = pltpu.get_barrier_semaphore()
    for partner in partners:
        pl.semaphore_signal(barrier, inc=1, device_id=partner, device_id_type=MESH)

    def block(ref, index):
        return ref.at[pl.ds(3 * index, 3)]

    own_row = x * 4 + zh * 2 + c
    own_rep = y * 4 + zl

    early = []
    for h in range(HALVES):
        early.append(
            pltpu.make_async_copy(
                feat_hbm.at[:, :, pl.ds(h * TILE, TILE)], block(feats[h], own_row), late_sem.at[h]
            )
        )
    loads = []
    for i in range(16):
        piece = pl.ds(3 * i, 3)
        loads.append(pltpu.make_async_copy(counts_hbm.at[piece], raw.at[piece], load_sem.at[i]))
    late = [
        pltpu.make_async_copy(weight_hbm, weight, late_sem.at[2]),
        pltpu.make_async_copy(cot_hbm, cot, late_sem.at[3]),
    ]
    for copy in early + loads + late:
        copy.start()
    out = []

    def put(src, dst, slot):
        copy = pltpu.make_async_copy(src, dst, late_sem.at[slot])
        copy.start()
        out.append(copy)

    for copy in early:
        copy.wait()
    pl.semaphore_wait(barrier, len(partners))

    def gather_z(h):
        mine = block(feats[h], own_row)
        send(("zh", h), mine, mine, to_zh)

    def gather_start(h):
        mine = block(feats[h], own_row)
        send(("xp", h), mine, mine, to_xp)
        send(("xm", h), mine, mine, to_xm)
        send(("c0", h), mine, mine, to_core)

    def row_index(x_, zh_):
        return x_ * 4 + zh_ * 2 + c

    def gather_near(h):
        arrived(("xp", h))
        left = block(feats[h], row_index(xm, zh))
        send(("xp2", h), left, left, to_xp)
        send(("c1", h), left, left, to_core)
        arrived(("xm", h))
        right = block(feats[h], row_index(xp, zh))
        send(("c2", h), right, right, to_core)

    def gather_far(h):
        arrived(("zh", h))
        other = block(feats[h], row_index(x, 1 - zh))
        send(("zxo", h), other, other, to_xo)
        send(("zxp", h), other, other, to_xp)
        send(("zxm", h), other, other, to_xm)
        send(("c3", h), other, other, to_core)

    def gather_near2(h):
        arrived(("xp2", h))
        oppo = block(feats[h], row_index(xo, zh))
        send(("c4", h), oppo, oppo, to_core)

    def gather_far2(h):
        for name, x_ in (("zxm", xp), ("zxp", xm), ("zxo", xo)):
            arrived((name, h))
            got = block(feats[h], row_index(x_, 1 - zh))
            send(("c" + name, h), got, got, to_core)

    def gather_end(h):
        for name in ("c0", "c1", "c2", "c3", "c4", "czxm", "czxp", "czxo"):
            arrived((name, h))

    def convert(first, end):
        for i in range(first, end):
            loads[i].wait()
            for t in range(3):
                total = None
                for k in range(3):
                    tile = raw[3 * i + t, k].astype(F32)
                    cnt[3 * i + t, :, k * TILE : (k + 1) * TILE] = tile.astype(BF16)
                    turned = tile.T
                    cnt_t[48 * k + 3 * i + t] = turned.astype(BF16)
                    part = jnp.sum(turned, axis=0, keepdims=True)
                    total = part if total is None else total + part
                deg_send[i // 4, i % 4, t : t + 1] = total

    def sort_tiles():
        side = 256
        line = jnp.concatenate(
            [cols_in[k] for k in range(3)] + [jnp.full((1, side - 144), 1000, jnp.int32)], axis=1
        )
        along = jnp.broadcast_to(line, (side, side))
        down = along.T
        at_row = lax.broadcasted_iota(jnp.int32, (side, side), 0)
        at_col = lax.broadcasted_iota(jnp.int32, (side, side), 1)
        less = (along < down).astype(jnp.int32)
        tied = ((along == down) & (at_col < at_row)).astype(jnp.int32)
        smaller = jnp.sum(less, axis=1, keepdims=True)
        rank = smaller + jnp.sum(tied, axis=1, keepdims=True)
        here = (rank == at_col).astype(jnp.int32)
        entry = at_row
        block_row = at_row - 48 * ((at_row >= 48).astype(jnp.int32) + (at_row >= 96).astype(jnp.int32))
        first = jnp.broadcast_to((smaller == rank).astype(jnp.int32), (side, side))

        def total(value):
            return jnp.sum(value, axis=0, keepdims=True)

        upto = total((down <= at_col).astype(jnp.int32))
        below = total((down < at_col).astype(jnp.int32))
        order_v[0:1] = total(here * entry)
        order_v[1:2] = total(here * block_row)
        order_v[2:3] = jnp.maximum(upto - 1, 0)
        flag_v[0:1] = 1.0 - total(here * first).astype(F32)
        flag_v[1:2] = jnp.minimum(upto - below, 1).astype(F32)
        for src, dst, slot in ((order_v, order, 4), (flag_v, flag, 5)):
            put(src, dst, slot)

    def sort_end():
        for copy in out:
            copy.wait()
        out.clear()

    def forward(part, target, own=False):
        h, t0, nt = part

        def step(i, carry):
            which, t = i // nt, t0 + i % nt
            r = target * 12 + which * 3 + t
            picked = jnp.concatenate([feats[h][cols[k, 0, r]] for k in range(3)], axis=0)
            total = jnp.dot(cnt[r], picked, preferred_element_type=F32)
            if own:
                pown[h, which, t] = total
            else:
                psend[h][target * 4 + which, t] = total.astype(BF16)
            return carry

        lax.fori_loop(0, 4 * nt, step, 0, unroll=4 * nt)

    def pair(part, target, which):
        h, t0, nt = part
        return psend[h].at[pl.ds(target * 4 + 2 * which, 2), pl.ds(t0, nt)]

    def add_into(ref, where, other):
        ref[where] = (ref[where].astype(F32) + other.astype(F32)).astype(BF16)

    def relay_in(part, way):
        h, t0, nt = part
        return yrel.at[h, way, :, pl.ds(t0, nt)]

    def final_in(part, way, which):
        h, t0, nt = part
        return yfin.at[h, way, pl.ds(2 * which, 2), pl.ds(t0, nt)]

    def reduce_start(part):
        forward(part, yo)
        send(("yr0", part), pair(part, yo, 0), relay_in(part, 0), to_yp)
        send(("yr1", part), pair(part, yo, 1), relay_in(part, 1), to_ym)

    def reduce_near(part):
        forward(part, yp)
        send(("yu0", part), pair(part, yp, 1), final_in(part, 0, 1), to_yp)
        forward(part, ym)
        send(("yu1", part), pair(part, ym, 0), final_in(part, 1, 0), to_ym)

    def reduce_own(part):
        forward(part, y, own=True)

    def reduce_relay(part):
        h, t0, nt = part
        tiles = pl.ds(t0, nt)
        arrived(("yr0", part))
        add_into(psend[h], (pl.ds(yp * 4, 2), tiles), yrel[h, 0, :, tiles])
        send(("yc0", part), pair(part, yp, 0), final_in(part, 0, 0), to_yp)
        arrived(("yr1", part))
        add_into(psend[h], (pl.ds(ym * 4 + 2, 2), tiles), yrel[h, 1, :, tiles])
        send(("yc1", part), pair(part, ym, 1), final_in(part, 1, 1), to_ym)

    def reduce_z(part):
        h, t0, nt = part
        tiles = pl.ds(t0, nt)
        for name in ("yu0", "yu1", "yc0", "yc1"):
            arrived((name, part))
        for which in range(4):
            total = (
                pown[h, which, tiles]
                + yfin[h, 0, which, tiles].astype(F32)
                + yfin[h, 1, which, tiles].astype(F32)
            )
            zown[h, which, tiles] = total
            zsend[h, which, tiles] = total.astype(BF16)
        for d in (2, 1, 3):
            send(
                ("rz%d" % d, part), zsend.at[h, zn[d], tiles], zrecv.at[h, zl, tiles], to_z[d]
            )

    def degree_start():
        deg_y[y] = deg_send[y]
        for name, target, index in (("dp", to_yp, yp), ("dm", to_ym, ym), ("do", to_yo, yo)):
            send(name, deg_send.at[index], deg_y.at[y], target)

    def degree_z():
        for name in ("dp", "dm", "do"):
            arrived(name)
        deg_zs[...] = deg_y[0] + deg_y[1] + deg_y[2] + deg_y[3]
        deg_z[zl] = deg_zs[zl]
        for d in (1, 2, 3):
            send("dz%d" % d, deg_zs.at[zn[d]], deg_z.at[zl], to_z[d])

    def degree_end():
        for d in (1, 2, 3):
            arrived("dz%d" % d)
        total = deg_z[0] + deg_z[1] + deg_z[2] + deg_z[3]
        return lax.rsqrt(1.0 + total)

    def split(value):
        high = value.astype(BF16)
        return high, (value - high.astype(F32)).astype(BF16)

    def dense_wait(part):
        for d in (1, 2, 3):
            arrived(("rz%d" % d, part))

    def dense(scale, first, end):
        for t in range(first, end):
            column = jnp.broadcast_to(scale[t : t + 1], (TILE, TILE)).T
            halves = []
            for h in range(HALVES):
                total = zown[h, zl, t]
                for d in (1, 2, 3):
                    total = total + zrecv[h, zn[d], t].astype(F32)
                halves.append(total * column)
            high, low = split(jnp.concatenate(halves, axis=1))
            rows = pl.ds(t * TILE, TILE)
            agg[rows] = high
            preact = jnp.dot(high, weight[...], preferred_element_type=F32) + jnp.dot(
                low, weight[...], preferred_element_type=F32
            )
            gate = jax.nn.sigmoid(preact)
            act[rows] = (preact * gate).astype(BF16)
            grad = cot[rows].astype(F32) * gate * (1.0 + preact * (1.0 - gate))
            high, low = split(grad)
            gpre[rows] = high
            turned = (((1,), (1,)), ((), ()))
            back = lax.dot_general(
                high, weight[...], turned, preferred_element_type=F32
            ) + lax.dot_general(low, weight[...], turned, preferred_element_type=F32)
            for h in range(HALVES):
                piece = back[:, h * TILE : (h + 1) * TILE] * column
                slab[h][3 * own_rep + t] = piece.astype(BF16)

    def dense_end():
        put(act, act_hbm, 6)

    def chunk(part, index):
        h, t0, nt = part
        return slab[h].at[pl.ds(3 * index + t0, nt)]

    def spread_start(part):
        mine = chunk(part, own_rep)
        for d in (2, 1, 3):
            send(("sz%d" % d, part), mine, mine, to_z[d])
        send(("sp0", part), mine, mine, to_yp)
        send(("sm0", part), mine, mine, to_ym)

    def spread_z(part, d):
        arrived(("sz%d" % d, part))
        got = chunk(part, y * 4 + zn[4 - d])
        send(("sp%d" % d, part), got, got, to_yp)
        send(("sm%d" % d, part), got, got, to_ym)

    def spread_y(part, d):
        source = zl if d == 0 else zn[4 - d]
        arrived(("sp%d" % d, part))
        if d % 2 == 0:
            got = chunk(part, ym * 4 + source)
            send(("sf%d" % d, part), got, got, to_yp)
        arrived(("sm%d" % d, part))
        if d % 2 == 1:
            got = chunk(part, yp * 4 + source)
            send(("sf%d" % d, part), got, got, to_ym)

    def spread_end(part):
        for d in range(4):
            arrived(("sf%d" % d, part))

    def backward(h, first, end):
        def step(i, carry):
            part = jnp.dot(
                cnt_t[order[0, i]], slab[h][order[1, i]], preferred_element_type=F32
            )
            total = acc[...] * flag[0, i] + part
            acc[...] = total
            prefix[i] = total.astype(BF16)
            return carry

        lax.fori_loop(first, end, step, 0, unroll=12)

    def collect(h):
        def step(i, carry):
            for t in range(3):
                j = 3 * i + t
                tile = prefix[order[2, j]].astype(F32) * flag[1, j]
                cout[h][i // 4, (i // 2) % 2, i % 2, t] = tile.astype(BF16)
            return carry

        lax.fori_loop(0, 16, step, 0, unroll=4)

    planes = (1 - zh, zh)

    def core_start(h):
        for n, plane in enumerate(planes):
            send(
                ("k%d" % n, h), cout[h].at[:, plane, 1 - c], corer.at[h, plane], to_core
            )

    def cross_start(h, n):
        plane = planes[n]
        arrived(("k%d" % n, h))
        total = cout[h][:, plane, c].astype(F32) + corer[h, plane].astype(F32)
        xs[h, plane] = total.astype(BF16)
        xown[h, n] = cout[h][x, plane, c].astype(F32) + corer[h, plane, x].astype(F32)
        for way, target, x_ in ((2, to_xo, xo), (0, to_xp, xp), (1, to_xm, xm)):
            send(("x%d%d" % (way, n), h), xs.at[h, plane, x_], xfin.at[h, n, way], target)

    def cross_sum(h, n):
        for way in (0, 1, 2):
            arrived(("x%d%d" % (way, n), h))
        total = xown[h, n]
        for way in range(3):
            total = total + xfin[h, n, way].astype(F32)
        return total

    def cross_z(h):
        zfs[h] = cross_sum(h, 0).astype(BF16)
        send(("fz", h), zfs.at[h], zfr.at[h], to_zh)

    def cross_own(h):
        keep[h] = cross_sum(h, 1)

    def cross_end(h):
        arrived(("fz", h))
        total = keep[h] + zfr[h].astype(F32)
        gf[h] = total.astype(BF16)
        put(gf.at[h], gf_hbm.at[:, :, pl.ds(h * TILE, TILE)], 8 + h)

    def gw_start():
        part = lax.dot_general(
            agg[...], gpre[...], (((0,), (0,)), ((), ())), preferred_element_type=F32
        )
        wp[...] = part.reshape(2, 4, 2, 16, 256)
        send("gc", wp.at[1 - c], g_core, to_core)

    def gw_x():
        arrived("gc")
        g1[...] = wp[c] + g_core[...]
        g_x[x] = g1[x]
        for name, target, x_ in (("gxp", to_xp, xp), ("gxm", to_xm, xm), ("gxo", to_xo, xo)):
            send(name, g1.at[x_], g_x.at[x], target)

    def gw_zh():
        for name in ("gxp", "gxm", "gxo"):
            arrived(name)
        g2[...] = g_x[0] + g_x[1] + g_x[2] + g_x[3]
        send("gzh", g2.at[1 - zh], g_zh, to_zh)

    def gw_y():
        arrived("gzh")
        g3[...] = g2[zh] + g_zh[...]
        g_y[y] = g3[...]
        for name, target in (("gyp", to_yp), ("gym", to_ym), ("gyo", to_yo)):
            send(name, g3, g_y.at[y], target)

    def gw_zl():
        for name in ("gyp", "gym", "gyo"):
            arrived(name)
        g4[...] = g_y[0] + g_y[1] + g_y[2] + g_y[3]
        g_zl[zl] = g4[...]
        for d in (1, 2, 3):
            send("gzl%d" % d, g4, g_zl.at[zl], to_z[d])

    def gw_back_zh():
        for d in (1, 2, 3):
            arrived("gzl%d" % d)
        gw_full[c, x, zh] = g_zl[0] + g_zl[1] + g_zl[2] + g_zl[3]
        mine = gw_full.at[c, x, zh]
        send("bzh", mine, mine, to_zh)

    def gw_back_x():
        arrived("bzh")
        mine = gw_full.at[c, x]
        for name, target in (("bxp", to_xp), ("bxm", to_xm), ("bxo", to_xo)):
            send(name, mine, mine, target)

    def gw_back_core():
        for name in ("bxp", "bxm", "bxo"):
            arrived(name)
        mine = gw_full.at[c]
        send("bc", mine, mine, to_core)

    def gw_end():
        arrived("bc")
        put(gw_full, gw_hbm, 7)

    s0, s1, s2 = SUM_PARTS
    a0, a1, b0, b1 = SPREAD_PARTS
    gather_z(0)
    gather_start(0)
    convert(0, 5)
    gather_z(1)
    gather_start(1)
    convert(5, 10)
    gather_near(0)
    convert(10, 16)
    gather_far(0)
    gather_near2(0)
    gather_near(1)
    degree_start()
    gather_far(1)
    gather_near2(1)
    gather_far2(0)
    gather_end(0)
    reduce_start(s0)
    reduce_near(s0)
    gather_far2(1)
    reduce_own(s0)
    degree_z()
    reduce_relay(s0)
    gather_end(1)
    reduce_start(s1)
    reduce_near(s1)
    reduce_start(s2)
    reduce_own(s1)
    reduce_relay(s1)
    reduce_near(s2)
    reduce_own(s2)
    reduce_z(s0)
    reduce_relay(s2)
    sort_tiles()
    scale = degree_end()
    for copy in late:
        copy.wait()
    sort_end()
    acc[...] = jnp.zeros_like(acc)
    reduce_z(s1)
    dense_wait(s0)
    dense_wait(s1)
    dense(scale, 0, 1)
    spread_start(a0)
    spread_start(a1)
    reduce_z(s2)
    spread_y(a0, 0)
    spread_y(a1, 0)
    for d in (1, 2, 3):
        spread_z(a0, d)
        spread_z(a1, d)
    dense_wait(s2)
    dense(scale, 1, 3)
    spread_start(b0)
    spread_start(b1)
    dense_end()
    for d in (1, 2, 3):
        spread_y(a0, d)
        spread_y(a1, d)
    gw_start()
    spread_y(b0, 0)
    for d in (1, 2, 3):
        spread_z(b0, d)
    spread_y(b1, 0)
    gw_x()
    for d in (1, 2, 3):
        spread_z(b1, d)
    for d in (1, 2, 3):
        spread_y(b0, d)
    gw_zh()
    spread_end(a0)
    spread_end(a1)
    spread_end(b0)
    backward(0, 0, 36)
    spread_y(b1, 1)
    backward(0, 36, 72)
    spread_y(b1, 2)
    backward(0, 72, 108)
    spread_y(b1, 3)
    backward(0, 108, 144)
    collect(0)
    core_start(0)
    gw_y()
    spread_end(b1)
    backward(1, 0, 36)
    cross_start(0, 0)
    cross_start(0, 1)
    backward(1, 36, 72)
    gw_zl()
    backward(1, 72, 108)
    cross_z(0)
    backward(1, 108, 144)
    collect(1)
    core_start(1)
    cross_own(0)
    gw_back_zh()
    cross_start(1, 0)
    cross_start(1, 1)
    gw_back_x()
    cross_end(0)
    cross_z(1)
    gw_back_core()
    cross_own(1)
    gw_end()
    cross_end(1)
    for copy in sent.values():
        copy.wait_send()
    for copy in out:
        copy.wait()


def finish(act_in, gf_in, gw_in, act_out, gf_out, gw_out):
    act_out[...] = act_in[...]
    gf_out[...] = gf_in[...]
    gw_out[...] = gw_in[...]


def shards(features, weight, block_cols, edge_counts, cotangent):
    vmem = pl.BlockSpec(memory_space=pltpu.VMEM)
    smem = pl.BlockSpec(memory_space=pltpu.SMEM)
    anywhere = pl.BlockSpec(memory_space=pl.ANY)
    slab = pltpu.VMEM((48, TILE, TILE), BF16)

    def tiles(*lead, dtype=BF16):
        return pltpu.VMEM((*lead, TILE, TILE), dtype)

    def floats(*shape):
        return pltpu.VMEM(shape, F32)

    shapes = (
        jax.ShapeDtypeStruct((384, 256), BF16),
        jax.ShapeDtypeStruct((3, TILE, 256), BF16),
        jax.ShapeDtypeStruct((2, 4, 2, 16, 256), F32),
    )
    columns = jnp.transpose(block_cols, (2, 0, 1))
    results = pl.pallas_call(
        kernel,
        out_shape=shapes,
        in_specs=[smem, vmem] + [anywhere] * 4,
        out_specs=(anywhere,) * 3,
        scratch_shapes=[
            tiles(48, 3, dtype=jnp.int32),
            pltpu.VMEM((48, TILE, 3 * TILE), BF16),
            tiles(144),
            slab, slab, tiles(16, 3), tiles(16, 3),
            tiles(2, 4, 3, dtype=F32),
            tiles(2, 2, 2, 3),
            tiles(2, 2, 4, 3),
            tiles(2, 4, 3), tiles(2, 4, 3, dtype=F32), tiles(2, 4, 3),
            slab, slab,
            tiles(144),
            floats(TILE, TILE),
            tiles(4, 2, 2, 3), tiles(4, 2, 2, 3),
            tiles(2, 2, 4, 3), tiles(2, 2, 4, 3),
            tiles(2, 2, 3, dtype=F32),
            tiles(2, 2, 3, 3),
            tiles(2, 3, dtype=F32), tiles(2, 3), tiles(2, 3),
            floats(4, 4, 8, TILE), floats(4, 4, 8, TILE),
            floats(4, 8, TILE), floats(4, 8, TILE),
            pltpu.VMEM((256, 256), BF16),
            pltpu.VMEM((384, 256), BF16), pltpu.VMEM((384, 256), BF16),
            pltpu.VMEM((384, 256), BF16), pltpu.VMEM((384, 256), BF16),
            tiles(2, 3),
            floats(2, 4, 2, 16, 256),
            floats(4, 2, 16, 256), floats(4, 2, 16, 256),
            floats(4, 2, 16, 256), floats(2, 16, 256),
            floats(16, 256), floats(16, 256),
            floats(4, 16, 256), floats(16, 256),
            floats(4, 16, 256),
            floats(2, 4, 2, 16, 256),
            pltpu.VMEM((8, 256), jnp.int32), pltpu.VMEM((8, 256), F32),
            pltpu.SMEM((8, 256), jnp.int32), pltpu.SMEM((8, 256), F32),
            pltpu.SemaphoreType.DMA((16,)),
            pltpu.SemaphoreType.DMA((10,)),
            pltpu.SemaphoreType.DMA((MESSAGES,)),
            pltpu.SemaphoreType.DMA((MESSAGES,)),
        ],
        compiler_params=pltpu.CompilerParams(
            collective_id=0, has_side_effects=True, vmem_limit_bytes=62 << 20
        ),
        name="graph_layer",
    )(
        columns, columns, features[0].reshape(3, TILE, 256), weight, cotangent[0],
        edge_counts[0],
    )
    activated, grad_features, grad_weight = pl.pallas_call(
        finish,
        out_shape=shapes,
        in_specs=[vmem] * 3,
        out_specs=(vmem,) * 3,
        name="finish",
    )(*results)
    return (
        activated[None], grad_features.reshape(1, 384, 256), grad_weight.reshape(256, 256)
    )


def solution(mesh):
    placed = (
        P("rep", "row", None),
        P(),
        P("rep", "row", None),
        P("rep", "row", None, None, None),
        P("row", "rep", None),
    )
    return jax.shard_map(
        shards,
        mesh=mesh,
        in_specs=placed,
        out_specs=(P("row", "rep", None), P("rep", "row", None), P()),
        check_vma=False,
    )
```

```python
import jax
import jax.numpy as jnp
from jax import lax
from jax.experimental import pallas as pl
from jax.experimental.pallas import tpu as pltpu
from jax.sharding import PartitionSpec as P

BF16 = jnp.bfloat16
F32 = jnp.float32
MESH = pl.DeviceIdType.MESH
TILE = 128
HALVES = 2
MESSAGES = 192
SUM_PARTS = ((0, 0, 3), (1, 0, 1), (1, 1, 2))
SPREAD_PARTS = ((0, 0, 1), (1, 0, 1), (0, 1, 2), (1, 1, 2))


def kernel(
    cols, cols_in, feat_hbm, weight_hbm, cot_hbm, counts_hbm,
    act_hbm, gf_hbm, gw_hbm,
    raw, cnt, cnt_t, feats0, feats1, psend0, psend1, pown, yrel, yfin, zsend, zown, zrecv,
    slab0, slab1, prefix, acc, cout0, cout1, corer, xs, xown, xfin, keep, zfs, zfr,
    deg_send, deg_y, deg_zs, deg_z, weight, cot, act, agg, gpre, gf,
    wp, g_core, g1, g_x, g2, g_zh, g3, g_y, g4, g_zl, gw_full,
    order_v, flag_v, order, flag,
    load_sem, late_sem, send_sem, recv_sem,
):
    rep = lax.axis_index("rep")
    row = lax.axis_index("row")
    y, zl = rep // 4, rep % 4
    x, zh, c = row // 4, (row // 2) % 2, row % 2
    feats, psend, slab, cout = (
        (feats0, feats1), (psend0, psend1), (slab0, slab1), (cout0, cout1)
    )

    def device(x_=x, y_=y, zl_=zl, zh_=zh, c_=c):
        return (y_ * 4 + zl_, x_ * 4 + zh_ * 2 + c_)

    xp, xm, xo = (x + 1) % 4, (x + 3) % 4, (x + 2) % 4
    yp, ym, yo = (y + 1) % 4, (y + 3) % 4, (y + 2) % 4
    zn = [(zl + d) % 4 for d in range(4)]
    to_xp, to_xm, to_xo = device(x_=xp), device(x_=xm), device(x_=xo)
    to_yp, to_ym, to_yo = device(y_=yp), device(y_=ym), device(y_=yo)
    to_z = [None] + [device(zl_=zn[d]) for d in (1, 2, 3)]
    to_zh = device(zh_=1 - zh)
    to_core = device(c_=1 - c)
    partners = [to_xp, to_xm, to_xo, to_yp, to_ym, to_yo, *to_z[1:], to_zh, to_core]

    sent = {}

    def send(name, src, dst, target):
        slot = len(sent)
        copy = pltpu.make_async_remote_copy(
            src_ref=src, dst_ref=dst, send_sem=send_sem.at[slot], recv_sem=recv_sem.at[slot],
            device_id=target, device_id_type=MESH,
        )
        copy.start()
        sent[name] = copy

    settled = [0]

    def settle(upto):
        for copy in list(sent.values())[settled[0] : upto]:
            copy.wait_send()
        settled[0] = upto

    def arrived(name):
        sent[name].wait_recv()

    barrier = pltpu.get_barrier_semaphore()
    for partner in partners:
        pl.semaphore_signal(barrier, inc=1, device_id=partner, device_id_type=MESH)

    def block(ref, index):
        return ref.at[pl.ds(3 * index, 3)]

    own_row = x * 4 + zh * 2 + c
    own_rep = y * 4 + zl

    early = []
    for h in range(HALVES):
        early.append(
            pltpu.make_async_copy(
                feat_hbm.at[:, :, pl.ds(h * TILE, TILE)], block(feats[h], own_row), late_sem.at[h]
            )
        )
    loads = []
    for i in range(16):
        piece = pl.ds(3 * i, 3)
        loads.append(pltpu.make_async_copy(counts_hbm.at[piece], raw.at[piece], load_sem.at[i]))
    late = [
        pltpu.make_async_copy(weight_hbm, weight, late_sem.at[2]),
        pltpu.make_async_copy(cot_hbm, cot, late_sem.at[3]),
    ]
    for copy in early + loads + late:
        copy.start()
    out = []

    def put(src, dst, slot):
        copy = pltpu.make_async_copy(src, dst, late_sem.at[slot])
        copy.start()
        out.append(copy)

    for copy in early:
        copy.wait()
    pl.semaphore_wait(barrier, len(partners))

    def gather_z(h):
        mine = block(feats[h], own_row)
        send(("zh", h), mine, mine, to_zh)

    def gather_start(h):
        mine = block(feats[h], own_row)
        send(("xp", h), mine, mine, to_xp)
        send(("xm", h), mine, mine, to_xm)
        send(("c0", h), mine, mine, to_core)

    def row_index(x_, zh_):
        return x_ * 4 + zh_ * 2 + c

    def gather_near(h):
        arrived(("xp", h))
        left = block(feats[h], row_index(xm, zh))
        send(("xp2", h), left, left, to_xp)
        send(("c1", h), left, left, to_core)
        arrived(("xm", h))
        right = block(feats[h], row_index(xp, zh))
        send(("c2", h), right, right, to_core)

    def gather_far(h):
        arrived(("zh", h))
        other = block(feats[h], row_index(x, 1 - zh))
        send(("zxo", h), other, other, to_xo)
        send(("zxp", h), other, other, to_xp)
        send(("zxm", h), other, other, to_xm)
        send(("c3", h), other, other, to_core)

    def gather_near2(h):
        arrived(("xp2", h))
        oppo = block(feats[h], row_index(xo, zh))
        send(("c4", h), oppo, oppo, to_core)

    def gather_far2(h):
        for name, x_ in (("zxm", xp), ("zxp", xm), ("zxo", xo)):
            arrived((name, h))
            got = block(feats[h], row_index(x_, 1 - zh))
            send(("c" + name, h), got, got, to_core)

    def gather_end(h):
        for name in ("c0", "c1", "c2", "c3", "c4", "czxm", "czxp", "czxo"):
            arrived((name, h))

    def convert(first, end):
        for i in range(first, end):
            loads[i].wait()
            for t in range(3):
                total = None
                for k in range(3):
                    tile = raw[3 * i + t, k].astype(F32)
                    cnt[3 * i + t, :, k * TILE : (k + 1) * TILE] = tile.astype(BF16)
                    turned = tile.T
                    cnt_t[48 * k + 3 * i + t] = turned.astype(BF16)
                    part = jnp.sum(turned, axis=0, keepdims=True)
                    total = part if total is None else total + part
                deg_send[i // 4, i % 4, t : t + 1] = total

    def sort_tiles():
        side = 256
        line = jnp.concatenate(
            [cols_in[k] for k in range(3)] + [jnp.full((1, side - 144), 1000, jnp.int32)], axis=1
        )
        along = jnp.broadcast_to(line, (side, side))
        down = along.T
        at_row = lax.broadcasted_iota(jnp.int32, (side, side), 0)
        at_col = lax.broadcasted_iota(jnp.int32, (side, side), 1)
        less = (along < down).astype(jnp.int32)
        tied = ((along == down) & (at_col < at_row)).astype(jnp.int32)
        smaller = jnp.sum(less, axis=1, keepdims=True)
        rank = smaller + jnp.sum(tied, axis=1, keepdims=True)
        here = (rank == at_col).astype(jnp.int32)
        entry = at_row
        block_row = at_row - 48 * ((at_row >= 48).astype(jnp.int32) + (at_row >= 96).astype(jnp.int32))
        first = jnp.broadcast_to((smaller == rank).astype(jnp.int32), (side, side))

        def total(value):
            return jnp.sum(value, axis=0, keepdims=True)

        upto = total((down <= at_col).astype(jnp.int32))
        below = total((down < at_col).astype(jnp.int32))
        order_v[0:1] = total(here * entry)
        order_v[1:2] = total(here * block_row)
        order_v[2:3] = jnp.maximum(upto - 1, 0)
        flag_v[0:1] = 1.0 - total(here * first).astype(F32)
        flag_v[1:2] = jnp.minimum(upto - below, 1).astype(F32)
        for src, dst, slot in ((order_v, order, 4), (flag_v, flag, 5)):
            put(src, dst, slot)

    def sort_end():
        for copy in out:
            copy.wait()
        out.clear()

    def forward(part, target, own=False):
        h, t0, nt = part

        def step(i, carry):
            which, t = i // nt, t0 + i % nt
            r = target * 12 + which * 3 + t
            picked = jnp.concatenate([feats[h][cols[k, 0, r]] for k in range(3)], axis=0)
            total = jnp.dot(cnt[r], picked, preferred_element_type=F32)
            if own:
                pown[h, which, t] = total
            else:
                psend[h][target * 4 + which, t] = total.astype(BF16)
            return carry

        lax.fori_loop(0, 4 * nt, step, 0, unroll=4 * nt)

    def pair(part, target, which):
        h, t0, nt = part
        return psend[h].at[pl.ds(target * 4 + 2 * which, 2), pl.ds(t0, nt)]

    def add_into(ref, where, other):
        ref[where] = (ref[where].astype(F32) + other.astype(F32)).astype(BF16)

    def relay_in(part, way):
        h, t0, nt = part
        return yrel.at[h, way, :, pl.ds(t0, nt)]

    def final_in(part, way, which):
        h, t0, nt = part
        return yfin.at[h, way, pl.ds(2 * which, 2), pl.ds(t0, nt)]

    def reduce_start(part):
        forward(part, yo)
        send(("yr0", part), pair(part, yo, 0), relay_in(part, 0), to_yp)
        send(("yr1", part), pair(part, yo, 1), relay_in(part, 1), to_ym)

    def reduce_near(part):
        forward(part, yp)
        send(("yu0", part), pair(part, yp, 1), final_in(part, 0, 1), to_yp)
        forward(part, ym)
        send(("yu1", part), pair(part, ym, 0), final_in(part, 1, 0), to_ym)

    def reduce_own(part):
        forward(part, y, own=True)

    def reduce_relay(part):
        h, t0, nt = part
        tiles = pl.ds(t0, nt)
        arrived(("yr0", part))
        add_into(psend[h], (pl.ds(yp * 4, 2), tiles), yrel[h, 0, :, tiles])
        send(("yc0", part), pair(part, yp, 0), final_in(part, 0, 0), to_yp)
        arrived(("yr1", part))
        add_into(psend[h], (pl.ds(ym * 4 + 2, 2), tiles), yrel[h, 1, :, tiles])
        send(("yc1", part), pair(part, ym, 1), final_in(part, 1, 1), to_ym)

    def reduce_z(part):
        h, t0, nt = part
        tiles = pl.ds(t0, nt)
        for name in ("yu0", "yu1", "yc0", "yc1"):
            arrived((name, part))
        for which in range(4):
            total = (
                pown[h, which, tiles]
                + yfin[h, 0, which, tiles].astype(F32)
                + yfin[h, 1, which, tiles].astype(F32)
            )
            zown[h, which, tiles] = total
            zsend[h, which, tiles] = total.astype(BF16)
        for d in (2, 1, 3):
            send(
                ("rz%d" % d, part), zsend.at[h, zn[d], tiles], zrecv.at[h, zl, tiles], to_z[d]
            )

    def degree_start():
        deg_y[y] = deg_send[y]
        for name, target, index in (("dp", to_yp, yp), ("dm", to_ym, ym), ("do", to_yo, yo)):
            send(name, deg_send.at[index], deg_y.at[y], target)

    def degree_z():
        for name in ("dp", "dm", "do"):
            arrived(name)
        deg_zs[...] = deg_y[0] + deg_y[1] + deg_y[2] + deg_y[3]
        deg_z[zl] = deg_zs[zl]
        for d in (1, 2, 3):
            send("dz%d" % d, deg_zs.at[zn[d]], deg_z.at[zl], to_z[d])

    def degree_end():
        for d in (1, 2, 3):
            arrived("dz%d" % d)
        total = deg_z[0] + deg_z[1] + deg_z[2] + deg_z[3]
        return lax.rsqrt(1.0 + total)

    def split(value):
        high = value.astype(BF16)
        return high, (value - high.astype(F32)).astype(BF16)

    def dense_wait(part):
        for d in (1, 2, 3):
            arrived(("rz%d" % d, part))

    def dense(scale, first, end):
        for t in range(first, end):
            column = jnp.broadcast_to(scale[t : t + 1], (TILE, TILE)).T
            halves = []
            for h in range(HALVES):
                total = zown[h, zl, t]
                for d in (1, 2, 3):
                    total = total + zrecv[h, zn[d], t].astype(F32)
                halves.append(total * column)
            high, low = split(jnp.concatenate(halves, axis=1))
            rows = pl.ds(t * TILE, TILE)
            agg[rows] = high
            preact = jnp.dot(high, weight[...], preferred_element_type=F32) + jnp.dot(
                low, weight[...], preferred_element_type=F32
            )
            gate = jax.nn.sigmoid(preact)
            act[rows] = (preact * gate).astype(BF16)
            grad = cot[rows].astype(F32) * gate * (1.0 + preact * (1.0 - gate))
            high, low = split(grad)
            gpre[rows] = high
            turned = (((1,), (1,)), ((), ()))
            back = lax.dot_general(
                high, weight[...], turned, preferred_element_type=F32
            ) + lax.dot_general(low, weight[...], turned, preferred_element_type=F32)
            for h in range(HALVES):
                piece = back[:, h * TILE : (h + 1) * TILE] * column
                slab[h][3 * own_rep + t] = piece.astype(BF16)

    def dense_end():
        put(act, act_hbm, 6)

    def chunk(part, index):
        h, t0, nt = part
        return slab[h].at[pl.ds(3 * index + t0, nt)]

    def spread_start(part):
        mine = chunk(part, own_rep)
        for d in (2, 1, 3):
            send(("sz%d" % d, part), mine, mine, to_z[d])
        send(("sp0", part), mine, mine, to_yp)
        send(("sm0", part), mine, mine, to_ym)

    def spread_z(part, d):
        arrived(("sz%d" % d, part))
        got = chunk(part, y * 4 + zn[4 - d])
        send(("sp%d" % d, part), got, got, to_yp)
        send(("sm%d" % d, part), got, got, to_ym)

    def spread_y(part, d):
        source = zl if d == 0 else zn[4 - d]
        arrived(("sp%d" % d, part))
        if d % 2 == 0:
            got = chunk(part, ym * 4 + source)
            send(("sf%d" % d, part), got, got, to_yp)
        arrived(("sm%d" % d, part))
        if d % 2 == 1:
            got = chunk(part, yp * 4 + source)
            send(("sf%d" % d, part), got, got, to_ym)

    def spread_end(part):
        for d in range(4):
            arrived(("sf%d" % d, part))

    def backward(h, first, end):
        def step(i, carry):
            part = jnp.dot(
                cnt_t[order[0, i]], slab[h][order[1, i]], preferred_element_type=F32
            )
            total = acc[...] * flag[0, i] + part
            acc[...] = total
            prefix[i] = total.astype(BF16)
            return carry

        lax.fori_loop(first, end, step, 0, unroll=12)

    def collect(h):
        def step(i, carry):
            for t in range(3):
                j = 3 * i + t
                tile = prefix[order[2, j]].astype(F32) * flag[1, j]
                cout[h][i // 4, (i // 2) % 2, i % 2, t] = tile.astype(BF16)
            return carry

        lax.fori_loop(0, 16, step, 0, unroll=4)

    planes = (1 - zh, zh)

    def core_start(h):
        for n, plane in enumerate(planes):
            send(
                ("k%d" % n, h), cout[h].at[:, plane, 1 - c], corer.at[h, plane], to_core
            )

    def cross_start(h, n):
        plane = planes[n]
        arrived(("k%d" % n, h))
        total = cout[h][:, plane, c].astype(F32) + corer[h, plane].astype(F32)
        xs[h, plane] = total.astype(BF16)
        xown[h, n] = cout[h][x, plane, c].astype(F32) + corer[h, plane, x].astype(F32)
        for way, target, x_ in ((2, to_xo, xo), (0, to_xp, xp), (1, to_xm, xm)):
            send(("x%d%d" % (way, n), h), xs.at[h, plane, x_], xfin.at[h, n, way], target)

    def cross_sum(h, n):
        for way in (0, 1, 2):
            arrived(("x%d%d" % (way, n), h))
        total = xown[h, n]
        for way in range(3):
            total = total + xfin[h, n, way].astype(F32)
        return total

    def cross_z(h):
        zfs[h] = cross_sum(h, 0).astype(BF16)
        send(("fz", h), zfs.at[h], zfr.at[h], to_zh)

    def cross_own(h):
        keep[h] = cross_sum(h, 1)

    def cross_end(h):
        arrived(("fz", h))
        total = keep[h] + zfr[h].astype(F32)
        gf[h] = total.astype(BF16)
        put(gf.at[h], gf_hbm.at[:, :, pl.ds(h * TILE, TILE)], 8 + h)

    def gw_start():
        part = lax.dot_general(
            agg[...], gpre[...], (((0,), (0,)), ((), ())), preferred_element_type=F32
        )
        wp[...] = part.reshape(2, 4, 2, 16, 256)
        send("gc", wp.at[1 - c], g_core, to_core)

    def gw_x():
        arrived("gc")
        g1[...] = wp[c] + g_core[...]
        g_x[x] = g1[x]
        for name, target, x_ in (("gxp", to_xp, xp), ("gxm", to_xm, xm), ("gxo", to_xo, xo)):
            send(name, g1.at[x_], g_x.at[x], target)

    def gw_zh():
        for name in ("gxp", "gxm", "gxo"):
            arrived(name)
        g2[...] = g_x[0] + g_x[1] + g_x[2] + g_x[3]
        send("gzh", g2.at[1 - zh], g_zh, to_zh)

    def gw_y():
        arrived("gzh")
        g3[...] = g2[zh] + g_zh[...]
        g_y[y] = g3[...]
        for name, target in (("gyp", to_yp), ("gym", to_ym), ("gyo", to_yo)):
            send(name, g3, g_y.at[y], target)

    def gw_zl():
        for name in ("gyp", "gym", "gyo"):
            arrived(name)
        g4[...] = g_y[0] + g_y[1] + g_y[2] + g_y[3]
        g_zl[zl] = g4[...]
        for d in (1, 2, 3):
            send("gzl%d" % d, g4, g_zl.at[zl], to_z[d])

    def gw_back_zh():
        for d in (1, 2, 3):
            arrived("gzl%d" % d)
        gw_full[c, x, zh] = g_zl[0] + g_zl[1] + g_zl[2] + g_zl[3]
        mine = gw_full.at[c, x, zh]
        send("bzh", mine, mine, to_zh)

    def gw_back_x():
        arrived("bzh")
        mine = gw_full.at[c, x]
        for name, target in (("bxp", to_xp), ("bxm", to_xm), ("bxo", to_xo)):
            send(name, mine, mine, target)

    def gw_back_core():
        for name in ("bxp", "bxm", "bxo"):
            arrived(name)
        mine = gw_full.at[c]
        send("bc", mine, mine, to_core)

    def gw_end():
        arrived("bc")
        put(gw_full, gw_hbm, 7)

    s0, s1, s2 = SUM_PARTS
    a0, a1, b0, b1 = SPREAD_PARTS
    gather_z(0)
    gather_start(0)
    convert(0,10)
    gather_near(0)
    gather_start(1)
    convert(10,16)
    gather_far(0)
    gather_z(1)
    gather_near2(0)
    gather_near(1)
    degree_start()
    gather_far2(0)
    gather_near2(1)
    gather_end(0)
    reduce_start(s0)
    reduce_near(s0)
    gather_far(1)
    reduce_own(s0)
    degree_z()
    gather_far2(1)
    reduce_relay(s0)
    gather_end(1)
    reduce_start(s1)
    reduce_near(s1)
    reduce_start(s2)
    reduce_own(s1)
    reduce_relay(s1)
    reduce_near(s2)
    reduce_own(s2)
    reduce_z(s0)
    reduce_relay(s2)
    sort_tiles()
    scale = degree_end()
    for copy in late:
        copy.wait()
    sort_end()
    acc[...] = jnp.zeros_like(acc)
    reduce_z(s1)
    reduce_z(s2)
    before_dense = len(sent)
    dense_wait(s0)
    dense_wait(s1)
    dense(scale, 0, 1)
    spread_start(a0)
    spread_start(a1)
    spread_y(a0, 0)
    spread_y(a1, 0)
    for d in (1, 2, 3):
        spread_z(a0, d)
        spread_z(a1, d)
    dense_wait(s2)
    dense(scale, 1, 3)
    spread_start(b0)
    spread_start(b1)
    dense_end()
    for d in (1, 2, 3):
        spread_y(a0, d)
        spread_y(a1, d)
    gw_start()
    spread_y(b0, 0)
    for d in (1, 2, 3):
        spread_z(b0, d)
    spread_y(b1, 0)
    gw_x()
    for d in (1, 2, 3):
        spread_z(b1, d)
    for d in (1, 2, 3):
        spread_y(b0, d)
    gw_zh()
    spread_end(a0)
    spread_end(a1)
    spread_end(b0)
    backward(0, 0, 36)
    spread_y(b1, 1)
    backward(0, 36, 72)
    spread_y(b1, 2)
    backward(0, 72, 108)
    spread_y(b1, 3)
    backward(0, 108, 144)
    collect(0)
    core_start(0)
    gw_y()
    spread_end(b1)
    backward(1, 0, 36)
    cross_start(0, 0)
    cross_start(0, 1)
    backward(1, 36, 72)
    gw_zl()
    backward(1, 72, 108)
    cross_z(0)
    backward(1, 108, 144)
    collect(1)
    core_start(1)
    cross_own(0)
    gw_back_zh()
    cross_start(1, 0)
    cross_start(1, 1)
    gw_back_x()
    cross_end(0)
    cross_z(1)
    gw_back_core()
    cross_own(1)
    gw_end()
    cross_end(1)
    settle(len(sent))
    for copy in out:
        copy.wait()


def finish(act_in, gf_in, gw_in, act_out, gf_out, gw_out):
    act_out[...] = act_in[...]
    gf_out[...] = gf_in[...]
    gw_out[...] = gw_in[...]


def shards(features, weight, block_cols, edge_counts, cotangent):
    vmem = pl.BlockSpec(memory_space=pltpu.VMEM)
    smem = pl.BlockSpec(memory_space=pltpu.SMEM)
    anywhere = pl.BlockSpec(memory_space=pl.ANY)
    slab = pltpu.VMEM((48, TILE, TILE), BF16)

    def tiles(*lead, dtype=BF16):
        return pltpu.VMEM((*lead, TILE, TILE), dtype)

    def floats(*shape):
        return pltpu.VMEM(shape, F32)

    shapes = (
        jax.ShapeDtypeStruct((384, 256), BF16),
        jax.ShapeDtypeStruct((3, TILE, 256), BF16),
        jax.ShapeDtypeStruct((2, 4, 2, 16, 256), F32),
    )
    columns = jnp.transpose(block_cols, (2, 0, 1))
    results = pl.pallas_call(
        kernel,
        out_shape=shapes,
        in_specs=[smem, vmem] + [anywhere] * 4,
        out_specs=(anywhere,) * 3,
        scratch_shapes=[
            tiles(48, 3, dtype=jnp.int32),
            pltpu.VMEM((48, TILE, 3 * TILE), BF16),
            tiles(144),
            slab, slab, tiles(16, 3), tiles(16, 3),
            tiles(2, 4, 3, dtype=F32),
            tiles(2, 2, 2, 3),
            tiles(2, 2, 4, 3),
            tiles(2, 4, 3), tiles(2, 4, 3, dtype=F32), tiles(2, 4, 3),
            slab, slab,
            tiles(144),
            floats(TILE, TILE),
            tiles(4, 2, 2, 3), tiles(4, 2, 2, 3),
            tiles(2, 2, 4, 3), tiles(2, 2, 4, 3),
            tiles(2, 2, 3, dtype=F32),
            tiles(2, 2, 3, 3),
            tiles(2, 3, dtype=F32), tiles(2, 3), tiles(2, 3),
            floats(4, 4, 8, TILE), floats(4, 4, 8, TILE),
            floats(4, 8, TILE), floats(4, 8, TILE),
            pltpu.VMEM((256, 256), BF16),
            pltpu.VMEM((384, 256), BF16), pltpu.VMEM((384, 256), BF16),
            pltpu.VMEM((384, 256), BF16), pltpu.VMEM((384, 256), BF16),
            tiles(2, 3),
            floats(2, 4, 2, 16, 256),
            floats(4, 2, 16, 256), floats(4, 2, 16, 256),
            floats(4, 2, 16, 256), floats(2, 16, 256),
            floats(16, 256), floats(16, 256),
            floats(4, 16, 256), floats(16, 256),
            floats(4, 16, 256),
            floats(2, 4, 2, 16, 256),
            pltpu.VMEM((8, 256), jnp.int32), pltpu.VMEM((8, 256), F32),
            pltpu.SMEM((8, 256), jnp.int32), pltpu.SMEM((8, 256), F32),
            pltpu.SemaphoreType.DMA((16,)),
            pltpu.SemaphoreType.DMA((10,)),
            pltpu.SemaphoreType.DMA((MESSAGES,)),
            pltpu.SemaphoreType.DMA((MESSAGES,)),
        ],
        compiler_params=pltpu.CompilerParams(
            collective_id=0, has_side_effects=True, vmem_limit_bytes=62 << 20
        ),
        name="graph_layer",
    )(
        columns, columns, features[0].reshape(3, TILE, 256), weight, cotangent[0],
        edge_counts[0],
    )
    activated, grad_features, grad_weight = pl.pallas_call(
        finish,
        out_shape=shapes,
        in_specs=[vmem] * 3,
        out_specs=(vmem,) * 3,
        name="finish",
    )(*results)
    return (
        activated[None], grad_features.reshape(1, 384, 256), grad_weight.reshape(256, 256)
    )


def solution(mesh):
    placed = (
        P("rep", "row", None),
        P(),
        P("rep", "row", None),
        P("rep", "row", None, None, None),
        P("row", "rep", None),
    )
    return jax.shard_map(
        shards,
        mesh=mesh,
        in_specs=placed,
        out_specs=(P("row", "rep", None), P("rep", "row", None), P()),
        check_vma=False,
    )
```

```python
import jax
import jax.numpy as jnp
from jax import lax
from jax.experimental import pallas as pl
from jax.experimental.pallas import tpu as pltpu
from jax.sharding import PartitionSpec as P

BF16 = jnp.bfloat16
F32 = jnp.float32
MESH = pl.DeviceIdType.MESH
TILE = 128
HALVES = 2
MESSAGES = 192
SUM_PARTS = ((0, 0, 3), (1, 0, 1), (1, 1, 2))
SPREAD_PARTS = ((0, 0, 1), (1, 0, 1), (0, 1, 2), (1, 1, 2))


def kernel(
    cols, cols_in, feat_hbm, weight_hbm, cot_hbm, counts_hbm,
    act_hbm, gf_hbm, gw_hbm,
    raw, cnt, cnt_t, feats0, feats1, psend0, psend1, pown, yrel, yfin, zsend, zown, zrecv,
    slab0, slab1, prefix, acc, cout0, cout1, corer, xs, xown, xfin, keep, zfs, zfr,
    deg_send, deg_y, deg_zs, deg_z, weight, cot, act, agg, gpre, gf,
    wp, g_core, g1, g_x, g2, g_zh, g3, g_y, g4, g_zl, gw_full,
    order_v, flag_v, order, flag,
    load_sem, late_sem, send_sem, recv_sem,
):
    rep = lax.axis_index("rep")
    row = lax.axis_index("row")
    y, zl = rep // 4, rep % 4
    x, zh, c = row // 4, (row // 2) % 2, row % 2
    feats, psend, slab, cout = (
        (feats0, feats1), (psend0, psend1), (slab0, slab1), (cout0, cout1)
    )

    def device(x_=x, y_=y, zl_=zl, zh_=zh, c_=c):
        return (y_ * 4 + zl_, x_ * 4 + zh_ * 2 + c_)

    xp, xm, xo = (x + 1) % 4, (x + 3) % 4, (x + 2) % 4
    yp, ym, yo = (y + 1) % 4, (y + 3) % 4, (y + 2) % 4
    zn = [(zl + d) % 4 for d in range(4)]
    to_xp, to_xm, to_xo = device(x_=xp), device(x_=xm), device(x_=xo)
    to_yp, to_ym, to_yo = device(y_=yp), device(y_=ym), device(y_=yo)
    to_z = [None] + [device(zl_=zn[d]) for d in (1, 2, 3)]
    to_zh = device(zh_=1 - zh)
    to_core = device(c_=1 - c)
    partners = [to_xp, to_xm, to_xo, to_yp, to_ym, to_yo, *to_z[1:], to_zh, to_core]

    sent = {}

    def send(name, src, dst, target):
        slot = len(sent)
        copy = pltpu.make_async_remote_copy(
            src_ref=src, dst_ref=dst, send_sem=send_sem.at[slot], recv_sem=recv_sem.at[slot],
            device_id=target, device_id_type=MESH,
        )
        copy.start()
        sent[name] = copy

    settled = [0]

    def settle(upto):
        for copy in list(sent.values())[settled[0] : upto]:
            copy.wait_send()
        settled[0] = upto

    def arrived(name):
        sent[name].wait_recv()

    barrier = pltpu.get_barrier_semaphore()
    for partner in partners:
        pl.semaphore_signal(barrier, inc=1, device_id=partner, device_id_type=MESH)

    def block(ref, index):
        return ref.at[pl.ds(3 * index, 3)]

    own_row = x * 4 + zh * 2 + c
    own_rep = y * 4 + zl

    early = []
    for h in range(HALVES):
        early.append(
            pltpu.make_async_copy(
                feat_hbm.at[:, :, pl.ds(h * TILE, TILE)], block(feats[h], own_row), late_sem.at[h]
            )
        )
    loads = []
    for i in range(16):
        piece = pl.ds(3 * i, 3)
        loads.append(pltpu.make_async_copy(counts_hbm.at[piece], raw.at[piece], load_sem.at[i]))
    late = [
        pltpu.make_async_copy(weight_hbm, weight, late_sem.at[2]),
        pltpu.make_async_copy(cot_hbm, cot, late_sem.at[3]),
    ]
    for copy in early + loads + late:
        copy.start()
    out = []

    def put(src, dst, slot):
        copy = pltpu.make_async_copy(src, dst, late_sem.at[slot])
        copy.start()
        out.append(copy)

    for copy in early:
        copy.wait()
    pl.semaphore_wait(barrier, len(partners))

    def gather_z(h):
        mine = block(feats[h], own_row)
        send(("zh", h), mine, mine, to_zh)

    def gather_start(h):
        mine = block(feats[h], own_row)
        send(("xp", h), mine, mine, to_xp)
        send(("xm", h), mine, mine, to_xm)
        send(("c0", h), mine, mine, to_core)

    def row_index(x_, zh_):
        return x_ * 4 + zh_ * 2 + c

    def gather_near(h):
        arrived(("xp", h))
        left = block(feats[h], row_index(xm, zh))
        send(("xp2", h), left, left, to_xp)
        send(("c1", h), left, left, to_core)
        arrived(("xm", h))
        right = block(feats[h], row_index(xp, zh))
        send(("c2", h), right, right, to_core)

    def gather_far(h):
        arrived(("zh", h))
        other = block(feats[h], row_index(x, 1 - zh))
        send(("zxo", h), other, other, to_xo)
        send(("zxp", h), other, other, to_xp)
        send(("zxm", h), other, other, to_xm)
        send(("c3", h), other, other, to_core)

    def gather_near2(h):
        arrived(("xp2", h))
        oppo = block(feats[h], row_index(xo, zh))
        send(("c4", h), oppo, oppo, to_core)

    def gather_far2(h):
        for name, x_ in (("zxm", xp), ("zxp", xm), ("zxo", xo)):
            arrived((name, h))
            got = block(feats[h], row_index(x_, 1 - zh))
            send(("c" + name, h), got, got, to_core)

    def gather_end(h):
        for name in ("c0", "c1", "c2", "c3", "c4", "czxm", "czxp", "czxo"):
            arrived((name, h))

    def convert(first, end):
        for i in range(first, end):
            loads[i].wait()
            for t in range(3):
                total = None
                for k in range(3):
                    tile = raw[3 * i + t, k].astype(F32)
                    cnt[3 * i + t, :, k * TILE : (k + 1) * TILE] = tile.astype(BF16)
                    turned = tile.T
                    cnt_t[48 * k + 3 * i + t] = turned.astype(BF16)
                    part = jnp.sum(turned, axis=0, keepdims=True)
                    total = part if total is None else total + part
                deg_send[i // 4, i % 4, t : t + 1] = total

    def sort_tiles():
        side = 256
        line = jnp.concatenate(
            [cols_in[k] for k in range(3)] + [jnp.full((1, side - 144), 1000, jnp.int32)], axis=1
        )
        along = jnp.broadcast_to(line, (side, side))
        down = along.T
        at_row = lax.broadcasted_iota(jnp.int32, (side, side), 0)
        at_col = lax.broadcasted_iota(jnp.int32, (side, side), 1)
        less = (along < down).astype(jnp.int32)
        tied = ((along == down) & (at_col < at_row)).astype(jnp.int32)
        smaller = jnp.sum(less, axis=1, keepdims=True)
        rank = smaller + jnp.sum(tied, axis=1, keepdims=True)
        here = (rank == at_col).astype(jnp.int32)
        entry = at_row
        block_row = at_row - 48 * ((at_row >= 48).astype(jnp.int32) + (at_row >= 96).astype(jnp.int32))
        first = jnp.broadcast_to((smaller == rank).astype(jnp.int32), (side, side))

        def total(value):
            return jnp.sum(value, axis=0, keepdims=True)

        upto = total((down <= at_col).astype(jnp.int32))
        below = total((down < at_col).astype(jnp.int32))
        order_v[0:1] = total(here * entry)
        order_v[1:2] = total(here * block_row)
        order_v[2:3] = jnp.maximum(upto - 1, 0)
        flag_v[0:1] = 1.0 - total(here * first).astype(F32)
        flag_v[1:2] = jnp.minimum(upto - below, 1).astype(F32)
        for src, dst, slot in ((order_v, order, 4), (flag_v, flag, 5)):
            put(src, dst, slot)

    def sort_end():
        for copy in out:
            copy.wait()
        out.clear()

    def forward(part, target, own=False):
        h, t0, nt = part

        def step(i, carry):
            which, t = i // nt, t0 + i % nt
            r = target * 12 + which * 3 + t
            picked = jnp.concatenate([feats[h][cols[k, 0, r]] for k in range(3)], axis=0)
            total = jnp.dot(cnt[r], picked, preferred_element_type=F32)
            if own:
                pown[h, which, t] = total
            else:
                psend[h][target * 4 + which, t] = total.astype(BF16)
            return carry

        lax.fori_loop(0, 4 * nt, step, 0, unroll=4 * nt)

    def pair(part, target, which):
        h, t0, nt = part
        return psend[h].at[pl.ds(target * 4 + 2 * which, 2), pl.ds(t0, nt)]

    def add_into(ref, where, other):
        ref[where] = (ref[where].astype(F32) + other.astype(F32)).astype(BF16)

    def relay_in(part, way):
        h, t0, nt = part
        return yrel.at[h, way, :, pl.ds(t0, nt)]

    def final_in(part, way, which):
        h, t0, nt = part
        return yfin.at[h, way, pl.ds(2 * which, 2), pl.ds(t0, nt)]

    def reduce_start(part):
        forward(part, yo)
        send(("yr0", part), pair(part, yo, 0), relay_in(part, 0), to_yp)
        send(("yr1", part), pair(part, yo, 1), relay_in(part, 1), to_ym)

    def reduce_near(part):
        forward(part, yp)
        send(("yu0", part), pair(part, yp, 1), final_in(part, 0, 1), to_yp)
        forward(part, ym)
        send(("yu1", part), pair(part, ym, 0), final_in(part, 1, 0), to_ym)

    def reduce_own(part):
        forward(part, y, own=True)

    def reduce_relay(part):
        h, t0, nt = part
        tiles = pl.ds(t0, nt)
        arrived(("yr0", part))
        add_into(psend[h], (pl.ds(yp * 4, 2), tiles), yrel[h, 0, :, tiles])
        send(("yc0", part), pair(part, yp, 0), final_in(part, 0, 0), to_yp)
        arrived(("yr1", part))
        add_into(psend[h], (pl.ds(ym * 4 + 2, 2), tiles), yrel[h, 1, :, tiles])
        send(("yc1", part), pair(part, ym, 1), final_in(part, 1, 1), to_ym)

    def reduce_z(part):
        h, t0, nt = part
        tiles = pl.ds(t0, nt)
        for name in ("yu0", "yu1", "yc0", "yc1"):
            arrived((name, part))
        for which in range(4):
            total = (
                pown[h, which, tiles]
                + yfin[h, 0, which, tiles].astype(F32)
                + yfin[h, 1, which, tiles].astype(F32)
            )
            zown[h, which, tiles] = total
            zsend[h, which, tiles] = total.astype(BF16)
        for d in (2, 1, 3):
            send(
                ("rz%d" % d, part), zsend.at[h, zn[d], tiles], zrecv.at[h, zl, tiles], to_z[d]
            )

    def degree_start():
        deg_y[y] = deg_send[y]
        for name, target, index in (("dp", to_yp, yp), ("dm", to_ym, ym), ("do", to_yo, yo)):
            send(name, deg_send.at[index], deg_y.at[y], target)

    def degree_z():
        for name in ("dp", "dm", "do"):
            arrived(name)
        deg_zs[...] = deg_y[0] + deg_y[1] + deg_y[2] + deg_y[3]
        deg_z[zl] = deg_zs[zl]
        for d in (1, 2, 3):
            send("dz%d" % d, deg_zs.at[zn[d]], deg_z.at[zl], to_z[d])

    def degree_end():
        for d in (1, 2, 3):
            arrived("dz%d" % d)
        total = deg_z[0] + deg_z[1] + deg_z[2] + deg_z[3]
        return lax.rsqrt(1.0 + total)

    def split(value):
        high = value.astype(BF16)
        return high, (value - high.astype(F32)).astype(BF16)

    def dense_wait(part):
        for d in (1, 2, 3):
            arrived(("rz%d" % d, part))

    def dense(scale, first, end):
        for t in range(first, end):
            column = jnp.broadcast_to(scale[t : t + 1], (TILE, TILE)).T
            halves = []
            for h in range(HALVES):
                total = zown[h, zl, t]
                for d in (1, 2, 3):
                    total = total + zrecv[h, zn[d], t].astype(F32)
                halves.append(total * column)
            high, low = split(jnp.concatenate(halves, axis=1))
            rows = pl.ds(t * TILE, TILE)
            agg[rows] = high
            preact = jnp.dot(high, weight[...], preferred_element_type=F32) + jnp.dot(
                low, weight[...], preferred_element_type=F32
            )
            gate = jax.nn.sigmoid(preact)
            act[rows] = (preact * gate).astype(BF16)
            grad = cot[rows].astype(F32) * gate * (1.0 + preact * (1.0 - gate))
            high, low = split(grad)
            gpre[rows] = high
            turned = (((1,), (1,)), ((), ()))
            back = lax.dot_general(
                high, weight[...], turned, preferred_element_type=F32
            ) + lax.dot_general(low, weight[...], turned, preferred_element_type=F32)
            for h in range(HALVES):
                piece = back[:, h * TILE : (h + 1) * TILE] * column
                slab[h][3 * own_rep + t] = piece.astype(BF16)

    def dense_end():
        put(act, act_hbm, 6)

    def chunk(part, index):
        h, t0, nt = part
        return slab[h].at[pl.ds(3 * index + t0, nt)]

    def spread_start(part):
        mine = chunk(part, own_rep)
        send(("sp0", part), mine, mine, to_yp)
        send(("sm0", part), mine, mine, to_ym)
        for d in (2, 1, 3):
            send(("sz%d" % d, part), mine, mine, to_z[d])

    def spread_z(part, d):
        arrived(("sz%d" % d, part))
        got = chunk(part, y * 4 + zn[4 - d])
        send(("sp%d" % d, part), got, got, to_yp)
        send(("sm%d" % d, part), got, got, to_ym)

    def spread_y(part, d):
        source = zl if d == 0 else zn[4 - d]
        arrived(("sp%d" % d, part))
        if d % 2 == 0:
            got = chunk(part, ym * 4 + source)
            send(("sf%d" % d, part), got, got, to_yp)
        arrived(("sm%d" % d, part))
        if d % 2 == 1:
            got = chunk(part, yp * 4 + source)
            send(("sf%d" % d, part), got, got, to_ym)

    def spread_end(part):
        for d in range(4):
            arrived(("sf%d" % d, part))

    def backward(h, first, end):
        def step(i, carry):
            part = jnp.dot(
                cnt_t[order[0, i]], slab[h][order[1, i]], preferred_element_type=F32
            )
            total = acc[...] * flag[0, i] + part
            acc[...] = total
            prefix[i] = total.astype(BF16)
            return carry

        lax.fori_loop(first, end, step, 0, unroll=12)

    def collect(h):
        def step(i, carry):
            for t in range(3):
                j = 3 * i + t
                tile = prefix[order[2, j]].astype(F32) * flag[1, j]
                cout[h][i // 4, (i // 2) % 2, i % 2, t] = tile.astype(BF16)
            return carry

        lax.fori_loop(0, 16, step, 0, unroll=4)

    planes = (1 - zh, zh)

    def core_start(h):
        for n, plane in enumerate(planes):
            send(
                ("k%d" % n, h), cout[h].at[:, plane, 1 - c], corer.at[h, plane], to_core
            )

    def cross_start(h, n):
        plane = planes[n]
        arrived(("k%d" % n, h))
        total = cout[h][:, plane, c].astype(F32) + corer[h, plane].astype(F32)
        xs[h, plane] = total.astype(BF16)
        xown[h, n] = cout[h][x, plane, c].astype(F32) + corer[h, plane, x].astype(F32)
        for way, target, x_ in ((2, to_xo, xo), (0, to_xp, xp), (1, to_xm, xm)):
            send(("x%d%d" % (way, n), h), xs.at[h, plane, x_], xfin.at[h, n, way], target)

    def cross_sum(h, n):
        for way in (0, 1, 2):
            arrived(("x%d%d" % (way, n), h))
        total = xown[h, n]
        for way in range(3):
            total = total + xfin[h, n, way].astype(F32)
        return total

    def cross_z(h):
        zfs[h] = cross_sum(h, 0).astype(BF16)
        send(("fz", h), zfs.at[h], zfr.at[h], to_zh)

    def cross_own(h):
        keep[h] = cross_sum(h, 1)

    def cross_end(h):
        arrived(("fz", h))
        total = keep[h] + zfr[h].astype(F32)
        gf[h] = total.astype(BF16)
        put(gf.at[h], gf_hbm.at[:, :, pl.ds(h * TILE, TILE)], 8 + h)

    def gw_start():
        part = lax.dot_general(
            agg[...], gpre[...], (((0,), (0,)), ((), ())), preferred_element_type=F32
        )
        wp[...] = part.reshape(2, 4, 2, 16, 256)
        send("gc", wp.at[1 - c], g_core, to_core)

    def gw_x():
        arrived("gc")
        g1[...] = wp[c] + g_core[...]
        g_x[x] = g1[x]
        for name, target, x_ in (("gxp", to_xp, xp), ("gxm", to_xm, xm), ("gxo", to_xo, xo)):
            send(name, g1.at[x_], g_x.at[x], target)

    def gw_zh():
        for name in ("gxp", "gxm", "gxo"):
            arrived(name)
        g2[...] = g_x[0] + g_x[1] + g_x[2] + g_x[3]
        send("gzh", g2.at[1 - zh], g_zh, to_zh)

    def gw_y():
        arrived("gzh")
        g3[...] = g2[zh] + g_zh[...]
        g_y[y] = g3[...]
        for name, target in (("gyp", to_yp), ("gym", to_ym), ("gyo", to_yo)):
            send(name, g3, g_y.at[y], target)

    def gw_zl():
        for name in ("gyp", "gym", "gyo"):
            arrived(name)
        g4[...] = g_y[0] + g_y[1] + g_y[2] + g_y[3]
        g_zl[zl] = g4[...]
        for d in (1, 2, 3):
            send("gzl%d" % d, g4, g_zl.at[zl], to_z[d])

    def gw_back_zh():
        for d in (1, 2, 3):
            arrived("gzl%d" % d)
        gw_full[c, x, zh] = g_zl[0] + g_zl[1] + g_zl[2] + g_zl[3]
        mine = gw_full.at[c, x, zh]
        send("bzh", mine, mine, to_zh)

    def gw_back_x():
        arrived("bzh")
        mine = gw_full.at[c, x]
        for name, target in (("bxp", to_xp), ("bxm", to_xm), ("bxo", to_xo)):
            send(name, mine, mine, target)

    def gw_back_core():
        for name in ("bxp", "bxm", "bxo"):
            arrived(name)
        mine = gw_full.at[c]
        send("bc", mine, mine, to_core)

    def gw_end():
        arrived("bc")
        put(gw_full, gw_hbm, 7)

    s0, s1, s2 = SUM_PARTS
    a0, a1, b0, b1 = SPREAD_PARTS
    gather_z(0)
    gather_start(0)
    convert(0,10)
    gather_near(0)
    gather_start(1)
    convert(10,16)
    gather_far(0)
    gather_z(1)
    gather_near2(0)
    gather_near(1)
    degree_start()
    gather_far2(0)
    gather_near2(1)
    gather_end(0)
    reduce_start(s0)
    reduce_near(s0)
    gather_far(1)
    reduce_own(s0)
    degree_z()
    reduce_relay(s0)
    gather_far2(1)
    gather_end(1)
    reduce_start(s1)
    reduce_near(s1)
    reduce_start(s2)
    reduce_own(s1)
    reduce_relay(s1)
    reduce_near(s2)
    reduce_own(s2)
    reduce_z(s0)
    reduce_relay(s2)
    sort_tiles()
    scale = degree_end()
    for copy in late:
        copy.wait()
    sort_end()
    acc[...] = jnp.zeros_like(acc)
    reduce_z(s1)
    reduce_z(s2)
    before_dense = len(sent)
    dense_wait(s0)
    dense_wait(s1)
    dense(scale, 0, 1)
    spread_start(a0)
    spread_start(a1)
    spread_y(a0, 0)
    spread_y(a1, 0)
    for d in (1, 2, 3):
        spread_z(a0, d)
        spread_z(a1, d)
    dense_wait(s2)
    dense(scale, 1, 3)
    spread_start(b0)
    spread_start(b1)
    dense_end()
    for d in (1, 2, 3):
        spread_y(a0, d)
        spread_y(a1, d)
    gw_start()
    spread_y(b0, 0)
    for d in (1, 2, 3):
        spread_z(b0, d)
    spread_y(b1, 0)
    gw_x()
    for d in (1, 2, 3):
        spread_z(b1, d)
    for d in (1, 2, 3):
        spread_y(b0, d)
    gw_zh()
    spread_end(a0)
    spread_end(a1)
    spread_end(b0)
    backward(0, 0, 36)
    spread_y(b1, 1)
    backward(0, 36, 72)
    spread_y(b1, 2)
    backward(0, 72, 108)
    spread_y(b1, 3)
    backward(0, 108, 144)
    collect(0)
    core_start(0)
    gw_y()
    spread_end(b1)
    backward(1, 0, 36)
    cross_start(0, 0)
    cross_start(0, 1)
    backward(1, 36, 72)
    gw_zl()
    backward(1, 72, 108)
    cross_z(0)
    backward(1, 108, 144)
    collect(1)
    core_start(1)
    cross_own(0)
    gw_back_zh()
    cross_start(1, 0)
    cross_start(1, 1)
    gw_back_x()
    cross_end(0)
    cross_z(1)
    gw_back_core()
    cross_own(1)
    gw_end()
    cross_end(1)
    settle(len(sent))
    for copy in out:
        copy.wait()


def finish(act_in, gf_in, gw_in, act_out, gf_out, gw_out):
    act_out[...] = act_in[...]
    gf_out[...] = gf_in[...]
    gw_out[...] = gw_in[...]


def shards(features, weight, block_cols, edge_counts, cotangent):
    vmem = pl.BlockSpec(memory_space=pltpu.VMEM)
    smem = pl.BlockSpec(memory_space=pltpu.SMEM)
    anywhere = pl.BlockSpec(memory_space=pl.ANY)
    slab = pltpu.VMEM((48, TILE, TILE), BF16)

    def tiles(*lead, dtype=BF16):
        return pltpu.VMEM((*lead, TILE, TILE), dtype)

    def floats(*shape):
        return pltpu.VMEM(shape, F32)

    shapes = (
        jax.ShapeDtypeStruct((384, 256), BF16),
        jax.ShapeDtypeStruct((3, TILE, 256), BF16),
        jax.ShapeDtypeStruct((2, 4, 2, 16, 256), F32),
    )
    columns = jnp.transpose(block_cols, (2, 0, 1))
    results = pl.pallas_call(
        kernel,
        out_shape=shapes,
        in_specs=[smem, vmem] + [anywhere] * 4,
        out_specs=(anywhere,) * 3,
        scratch_shapes=[
            tiles(48, 3, dtype=jnp.int32),
            pltpu.VMEM((48, TILE, 3 * TILE), BF16),
            tiles(144),
            slab, slab, tiles(16, 3), tiles(16, 3),
            tiles(2, 4, 3, dtype=F32),
            tiles(2, 2, 2, 3),
            tiles(2, 2, 4, 3),
            tiles(2, 4, 3), tiles(2, 4, 3, dtype=F32), tiles(2, 4, 3),
            slab, slab,
            tiles(144),
            floats(TILE, TILE),
            tiles(4, 2, 2, 3), tiles(4, 2, 2, 3),
            tiles(2, 2, 4, 3), tiles(2, 2, 4, 3),
            tiles(2, 2, 3, dtype=F32),
            tiles(2, 2, 3, 3),
            tiles(2, 3, dtype=F32), tiles(2, 3), tiles(2, 3),
            floats(4, 4, 8, TILE), floats(4, 4, 8, TILE),
            floats(4, 8, TILE), floats(4, 8, TILE),
            pltpu.VMEM((256, 256), BF16),
            pltpu.VMEM((384, 256), BF16), pltpu.VMEM((384, 256), BF16),
            pltpu.VMEM((384, 256), BF16), pltpu.VMEM((384, 256), BF16),
            tiles(2, 3),
            floats(2, 4, 2, 16, 256),
            floats(4, 2, 16, 256), floats(4, 2, 16, 256),
            floats(4, 2, 16, 256), floats(2, 16, 256),
            floats(16, 256), floats(16, 256),
            floats(4, 16, 256), floats(16, 256),
            floats(4, 16, 256),
            floats(2, 4, 2, 16, 256),
            pltpu.VMEM((8, 256), jnp.int32), pltpu.VMEM((8, 256), F32),
            pltpu.SMEM((8, 256), jnp.int32), pltpu.SMEM((8, 256), F32),
            pltpu.SemaphoreType.DMA((16,)),
            pltpu.SemaphoreType.DMA((10,)),
            pltpu.SemaphoreType.DMA((MESSAGES,)),
            pltpu.SemaphoreType.DMA((MESSAGES,)),
        ],
        compiler_params=pltpu.CompilerParams(
            collective_id=0, has_side_effects=True, vmem_limit_bytes=62 << 20
        ),
        name="graph_layer",
    )(
        columns, columns, features[0].reshape(3, TILE, 256), weight, cotangent[0],
        edge_counts[0],
    )
    activated, grad_features, grad_weight = pl.pallas_call(
        finish,
        out_shape=shapes,
        in_specs=[vmem] * 3,
        out_specs=(vmem,) * 3,
        name="finish",
    )(*results)
    return (
        activated[None], grad_features.reshape(1, 384, 256), grad_weight.reshape(256, 256)
    )


def solution(mesh):
    placed = (
        P("rep", "row", None),
        P(),
        P("rep", "row", None),
        P("rep", "row", None, None, None),
        P("row", "rep", None),
    )
    return jax.shard_map(
        shards,
        mesh=mesh,
        in_specs=placed,
        out_specs=(P("row", "rep", None), P("rep", "row", None), P()),
        check_vma=False,
    )
```
